512 devices in a mesh: feed: 32 (over z, x), tm: 16 (over y, core).
Axes of the slice: x: 4, y: 8, z: 8, core: 2. Of those that a mesh axis runs over, the one named last changes fastest.
Arguments:
- voltages: bfloat16 [2, 256, 64, 8192], P(None, 'feed', 'tm'), may hold values from -6 to 6
- channel_lag: int32 [8192], replicated, may hold values from 0 to 2
- offsets: int32 [5, 4096], replicated, may hold values from 0 to 1
Outputs:
- dedispersed: float32 [256, 32, 8192], P('feed', 'tm')
The draws below stay inside these ranges and needn't reach their ends.
All inputs are finite; a program needn't handle non-finite values.
Results may differ from the reference program's by a relative error of at most 0.00063.
Values may be sent and summed in bfloat16 or wider, within the bound.
No kernel may reach another device: no remote copies, remote signals or barrier semaphores. Data moves between devices by JAX's collectives and lax.ppermute only.
A program may use at most 192 MiB of HBM per device.

```python
import math
import jax
import jax.numpy as jnp
from jax import lax

FEEDS = 256
CH = 8192
DS = 2
SECTIONS = 5
T_DEV = 2
SAMPLES = 64
TIMES = 32
LAGMAX = 2


def with_ends(result, key, smallest, top_value):
    shape = result.shape
    index_at = [jax.random.randint(jax.random.fold_in(key, axis), (), 0, shape[axis]) for axis in range(len(shape))]
    result = result.at[tuple(index_at)].set(smallest)
    longest = shape.index(max(shape))
    index_at[longest] = (index_at[longest] + 1) % shape[longest]
    return result.at[tuple(index_at)].set(top_value)


def shard_levels(rng, dims, pieces, smallest, largest):
    factor_of, own = 1.0, jax.random.fold_in(rng, 6)
    for dim, blocks in pieces:
        draws = jnp.exp(jax.random.uniform(jax.random.fold_in(own, dim), (blocks,), jnp.float32, smallest / len(pieces), largest / len(pieces)))
        factor_of = factor_of * jnp.repeat(draws, dims[dim] // blocks).reshape([-1 if axis == dim else 1 for axis in range(len(dims))])
    return factor_of


def bell_draw(stream_key, shape, scale, most, pieces=(), kind=jnp.bfloat16):
    level = shard_levels(stream_key, shape, pieces, -0.22, 0.18) if pieces else 1.0
    entries = jax.random.normal(stream_key, shape, jnp.float32) * scale * level
    return jnp.minimum(jnp.maximum(entries, -most), most).astype(kind)


def setup_inputs(seed: int = 0) -> dict:
    arg_keys = jax.random.split(jax.random.key(seed), 4)
    voltages = bell_draw(arg_keys[0], (2, FEEDS, SAMPLES, CH), 1.0, 6.0, ((1, 32), (2, 16)))
    channel_lag = with_ends(jax.random.randint(arg_keys[1], (CH,), 0, LAGMAX + 1), jax.random.fold_in(arg_keys[1], 1), 0, LAGMAX).astype(jnp.int32)
    offsets = with_ends(jax.random.randint(arg_keys[2], (SECTIONS, CH // 2), 0, T_DEV), jax.random.fold_in(arg_keys[2], 1), 0, T_DEV - 1).astype(jnp.int32)
    return {"voltages": voltages, "channel_lag": channel_lag, "offsets": offsets}


def beam_block(voltages, start, width):
    block = lax.dynamic_slice_in_dim(voltages, start, width, 3).astype(jnp.float32)
    field = lax.complex(block[0], block[1])
    spectrum = jnp.fft.fft(field, axis=0) / math.sqrt(FEEDS)
    power = spectrum.real * spectrum.real + spectrum.imag * spectrum.imag
    power = power.reshape(FEEDS, TIMES, DS, width).mean(axis=2)
    return power.astype(jnp.bfloat16)

def dedisperse_beam(intensity, channel_lag, offsets):
    padded = jnp.concatenate([jnp.zeros((LAGMAX, CH), intensity.dtype), intensity], axis=0)
    times_col = jnp.arange(TIMES, dtype=jnp.int32)[:, None]
    index = (LAGMAX + times_col - channel_lag[None, :]).astype(jnp.int32)
    level = jnp.take_along_axis(padded, index, axis=0).astype(jnp.float32)
    for section in range(SECTIONS):
        half = 2 ** section
        groups = CH // (2 * half)
        shaped = level.reshape(TIMES, groups, 2, half)
        lower = shaped[:, :, 0, :].reshape(TIMES, CH // 2)
        upper = shaped[:, :, 1, :].reshape(TIMES, CH // 2)
        upper_pad = jnp.concatenate([jnp.zeros((T_DEV, CH // 2), jnp.float32), upper], axis=0)
        first = (T_DEV + times_col - offsets[section][None, :]).astype(jnp.int32)
        new_low = lower + jnp.take_along_axis(upper_pad, first, axis=0)
        new_up = lower + jnp.take_along_axis(upper_pad, first - 1, axis=0)
        level = jnp.stack([new_low.reshape(TIMES, groups, half), new_up.reshape(TIMES, groups, half)], axis=2).reshape(TIMES, CH)
    return level * (1.0 / 2 ** SECTIONS)

def reference(voltages, channel_lag, offsets):
    width = math.gcd(CH, 512)
    starts = jnp.arange(CH // width, dtype=jnp.int32) * width
    blocks = lax.map(lambda start: beam_block(voltages, start, width), starts)
    intensity = jnp.transpose(blocks, (1, 2, 0, 3)).reshape(FEEDS, TIMES, CH)
    return lax.map(lambda beam_rows: dedisperse_beam(beam_rows, channel_lag, offsets), intensity)
```

```python
import functools
import math

import jax
import jax.numpy as jnp
import ml_dtypes
import numpy as np
from jax import lax
from jax.experimental import pallas as pl
from jax.experimental.pallas import tpu as pltpu
from jax.sharding import Mesh
from jax.sharding import PartitionSpec as P

DS = 2
SECTIONS = 5
GROUP = 2**SECTIONS
LANES = 128
VMEM_LIMIT = 48 * 1024 * 1024


def dft_tables(feeds):
    hi, big, low = np.meshgrid(np.arange(2), np.arange(feeds // 8), np.arange(4), indexing="ij")
    beam = (8 * big + 4 * hi + low).reshape(-1)
    feed = np.arange(feeds)
    angle = (beam[:, None] * feed[None, :] % feeds) * (2.0 * math.pi / feeds)
    cosine = np.cos(angle) / math.sqrt(feeds)
    sine = np.sin(angle) / math.sqrt(feeds)
    real = np.stack([cosine.reshape(feeds, -1, 8), sine.reshape(feeds, -1, 8)], axis=2)
    imag = np.stack([-sine.reshape(feeds, -1, 8), cosine.reshape(feeds, -1, 8)], axis=2)
    table = np.concatenate([real, imag], axis=0).reshape(2 * feeds, 2 * feeds)
    high = table.astype(ml_dtypes.bfloat16)
    rest = (table - high.astype(np.float64)).astype(ml_dtypes.bfloat16)
    return high, rest


def lane_index(shape):
    return lax.broadcasted_iota(jnp.int32, shape, len(shape) - 1)


def roll(x, by):
    return pltpu.roll(x, by % x.shape[-1], x.ndim - 1)


def swap_blocks(rows):
    lane = lane_index(rows[0].shape)
    low_half = lane < 64
    even = lane % 64 < 32
    mid = [None] * 4
    for n in range(2):
        mid[n] = jnp.where(low_half, rows[n], roll(rows[n + 2], 64))
        mid[n + 2] = jnp.where(low_half, roll(rows[n], 64), rows[n + 2])
    out = [None] * 4
    for n in (0, 2):
        out[n] = jnp.where(even, mid[n], roll(mid[n + 1], 32))
        out[n + 1] = jnp.where(even, roll(mid[n], -32), mid[n + 1])
    return out


def pack_kernel(x_ref, out_ref):
    tiles = x_ref.shape[2] // LANES
    for j in range(tiles):
        lanes = pl.ds(j * LANES, LANES)
        rows = [x_ref[n, :, lanes].astype(jnp.float32) for n in range(4)]
        for g, value in enumerate(swap_blocks(rows)):
            out_ref[4 * j + g] = value.astype(jnp.bfloat16)


def beam_kernel(high_ref, rest_ref, x_ref, out_ref):
    sources, several, cf, lanes = x_ref.shape
    x = jnp.concatenate(
        [x_ref[:, k].reshape(sources * cf, lanes) for k in range(several)], axis=1
    )
    beam = jnp.dot(high_ref[...], x, preferred_element_type=jnp.float32)
    beam = beam + jnp.dot(rest_ref[...], x, preferred_element_type=jnp.float32)
    feeds = beam.shape[0] // 2
    half = feeds // 2
    power = beam[:feeds] * beam[:feeds] + beam[feeds:] * beam[feeds:]
    even = lane_index((half, lanes)) % 64 < 32
    for k in range(several):
        first = power[:half, k * lanes : (k + 1) * lanes]
        second = power[half:, k * lanes : (k + 1) * lanes]
        total = jnp.where(even, first + roll(first, -32), second + roll(second, 32))
        out_ref[k] = (total * (1.0 / DS)).astype(jnp.bfloat16)


def mask_kernel(place_ref, lag_ref, off_ref, out_ref):
    place = place_ref[0]
    per_lag = LANES // GROUP
    lag = lag_ref[pl.ds(place // per_lag, 1), :].astype(jnp.float32)
    lag = jnp.broadcast_to(lag, (8, LANES))
    row = lax.broadcasted_iota(jnp.int32, (LANES, LANES), 0)
    lane = lane_index((LANES, LANES))
    channel = lane % GROUP
    source = (place % per_lag) * GROUP + channel
    pick = (row == source).astype(jnp.float32)
    out_ref[0] = jnp.dot(lag, pick, preferred_element_type=jnp.float32)
    half_group = GROUP // 2
    per_off = LANES // half_group
    for s in range(SECTIONS):
        h = 2**s
        values = off_ref[s, pl.ds(place // per_off, 1), :].astype(jnp.float32)
        values = jnp.broadcast_to(values, (8, LANES))
        pair = h * (channel // (2 * h)) + channel % h
        source = (place % per_off) * half_group + pair
        pick = (row == source).astype(jnp.float32)
        out_ref[s + 1] = jnp.dot(values, pick, preferred_element_type=jnp.float32)


def tree_kernel(core_ref, mask_ref, own_ref, other_ref, out_ref):
    blocks = own_ref.shape[0]
    rows = 16
    lane = lane_index((rows, LANES))
    first_time = lane < 64
    channel = lane % GROUP

    def wide(k):
        part = mask_ref[k]
        return jnp.concatenate([part] * (rows // 8), axis=0)

    zero = jnp.zeros((rows, LANES), jnp.float32)

    def back_one(even, odd):
        s_even, s_odd = [], []
        for y in range(blocks):
            before = odd[y - 1] if y else zero
            s_even.append(roll(jnp.where(first_time, even[y], before), 64))
            s_odd.append(roll(jnp.where(first_time, odd[y], even[y]), 64))
        return s_even, s_odd

    def run(is_odd):
        def step(k, _):
            at = pl.ds(pl.multiple_of(k * rows, rows), rows)
            mine = [own_ref[y, at, :].astype(jnp.float32) for y in range(blocks)]
            theirs = [other_ref[y, at, :].astype(jnp.float32) for y in range(blocks)]
            even, odd = (theirs, mine) if is_odd else (mine, theirs)
            lag = wide(0)
            s_even, s_odd = back_one(even, odd)

            def lagged(now, one, two):
                return jnp.where(lag == 0.0, now, jnp.where(lag == 1.0, one, two))

            new_even = [
                lagged(even[y], s_even[y], odd[y - 1] if y else zero) for y in range(blocks)
            ]
            new_odd = [lagged(odd[y], s_odd[y], even[y]) for y in range(blocks)]
            even, odd = new_even, new_odd
            for s in range(SECTIONS):
                h = 2**s
                off = wide(s + 1) > 0.5
                upper = (channel // h) % 2 == 1
                s_even, s_odd = back_one(even, odd)

                def combine(now, one, two):
                    nearer = jnp.where(off, one, now)
                    farther = jnp.where(off, two, one)
                    return jnp.where(upper, roll(now, h) + farther, now + roll(nearer, -h))

                last = s == SECTIONS - 1
                new_even = new_odd = None
                if not (last and is_odd):
                    new_even = [
                        combine(even[y], s_even[y], odd[y - 1] if y else zero)
                        for y in range(blocks)
                    ]
                if not (last and not is_odd):
                    new_odd = [combine(odd[y], s_odd[y], even[y]) for y in range(blocks)]
                even, odd = new_even, new_odd
            final = odd if is_odd else even
            per = rows // 4
            for y in range(blocks):
                value = final[y] * (1.0 / 2**SECTIONS)
                for q in range(per):
                    out_ref[k * per + q, y] = value[4 * q : 4 * q + 4]
            return 0

        lax.fori_loop(0, own_ref.shape[1] // rows, step, 0)

    @pl.when(core_ref[0] == 0)
    def _():
        run(False)

    @pl.when(core_ref[0] != 0)
    def _():
        run(True)


def unpack_kernel(x_ref, out_ref):
    tiles = x_ref.shape[0] // 2
    lane = lane_index((8, LANES))
    row = lax.broadcasted_iota(jnp.int32, (8, LANES), 0)
    low_half = lane < 64
    top = row < 4
    stay = top == (lane % 64 < 32)
    for j in range(tiles):
        v0 = x_ref[2 * j]
        v1 = x_ref[2 * j + 1]
        u = (jnp.where(low_half, v0, roll(v1, 64)), jnp.where(low_half, roll(v0, 64), v1))
        for t in range(2):
            crossed = pltpu.roll(u[t], 4, 0)
            moved = jnp.where(top, roll(crossed, 32), roll(crossed, -32))
            out_ref[t, :, pl.ds(j * LANES, LANES)] = jnp.where(stay, u[t], moved)


def on_device(high, rest, voltages, channel_lag, offsets):
    parts, local, samp, channels = voltages.shape
    feed_count = lax.axis_size("feed")
    y_count = lax.axis_size("y")
    peers = feed_count * y_count
    cf = parts * local
    params = pltpu.CompilerParams(vmem_limit_bytes=VMEM_LIMIT)
    vmem = pl.BlockSpec(memory_space=pltpu.VMEM)
    smem = pl.BlockSpec(memory_space=pltpu.SMEM)

    rows = voltages.reshape(cf, samp, channels).transpose(1, 0, 2)
    steps = 8
    width = channels // steps
    packed = pl.pallas_call(
        pack_kernel,
        grid=(steps,),
        in_specs=[pl.BlockSpec((samp, cf, width), lambda i: (0, 0, i))],
        out_specs=pl.BlockSpec((width // GROUP, cf, LANES), lambda i: (i, 0, 0)),
        out_shape=jax.ShapeDtypeStruct((peers, cf, LANES), jnp.bfloat16),
        compiler_params=params,
        name="pack",
    )(rows)
    turned = lax.all_to_all(packed, ("feed", "y"), split_axis=0, concat_axis=0, tiled=True)

    place = (lax.axis_index("feed") * y_count + lax.axis_index("y")).reshape(1)
    masks = pl.pallas_call(
        mask_kernel,
        in_specs=[smem, vmem, vmem],
        out_specs=vmem,
        out_shape=jax.ShapeDtypeStruct((SECTIONS + 1, 8, LANES), jnp.float32),
        name="masks",
    )(place, channel_lag.reshape(-1, LANES), offsets.reshape(SECTIONS, -1, LANES))

    several = 2
    beams = 2 * feed_count * local // 2
    turned = turned.reshape(feed_count, y_count, cf, LANES)
    whole = lambda i: (0, 0)
    own = pl.pallas_call(
        beam_kernel,
        grid=(y_count // several,),
        in_specs=[
            pl.BlockSpec(high.shape, whole),
            pl.BlockSpec(rest.shape, whole),
            pl.BlockSpec((feed_count, several, cf, LANES), lambda i: (0, i, 0, 0)),
        ],
        out_specs=pl.BlockSpec((several, beams // 2, LANES), lambda i: (i, 0, 0)),
        out_shape=jax.ShapeDtypeStruct((y_count, beams // 2, LANES), jnp.bfloat16),
        compiler_params=params,
        name="beams",
    )(high, rest, turned)
    other = lax.ppermute(own, "core", [(0, 1), (1, 0)])

    core = lax.axis_index("core").reshape(1)
    trials = pl.pallas_call(
        tree_kernel,
        in_specs=[smem, vmem, vmem, vmem],
        out_specs=vmem,
        out_shape=jax.ShapeDtypeStruct((feed_count, y_count, 4, LANES), jnp.float32),
        compiler_params=params,
        name="tree",
    )(core, masks, own, other)
    trials = trials.reshape(peers, 4, LANES)
    back = lax.all_to_all(trials, ("feed", "y"), split_axis=0, concat_axis=0, tiled=True)

    out = pl.pallas_call(
        unpack_kernel,
        grid=(steps,),
        in_specs=[pl.BlockSpec((peers // 2 // steps, 8, LANES), lambda i: (i, 0, 0))],
        out_specs=pl.BlockSpec((2, 8, width), lambda i: (0, 0, i)),
        out_shape=jax.ShapeDtypeStruct((2, 8, channels), jnp.float32),
        compiler_params=params,
        name="unpack",
    )(back.reshape(peers // 2, 8, LANES))
    return out.transpose(1, 0, 2)


def solution(mesh):
    devices = mesh.devices
    fine = Mesh(devices.reshape(devices.shape[0], -1, 2), ("feed", "y", "core"))
    high, rest = dft_tables(8 * devices.shape[0])
    times = ("y", "core")
    body = jax.shard_map(
        functools.partial(on_device),
        mesh=fine,
        in_specs=(P(), P(), P(None, "feed", times, None), P(), P()),
        out_specs=P("feed", times, None),
        check_vma=False,
    )

    def run(voltages, channel_lag, offsets):
        return body(jnp.asarray(high), jnp.asarray(rest), voltages, channel_lag, offsets)

    return run
```

```python
import functools
import math

import jax
import jax.numpy as jnp
import ml_dtypes
import numpy as np
from jax import lax
from jax.experimental import pallas as pl
from jax.experimental.pallas import tpu as pltpu
from jax.sharding import Mesh
from jax.sharding import PartitionSpec as P

DS = 2
SECTIONS = 5
GROUP = 2**SECTIONS
LANES = 128
TOP = 14.5
FINE = 800.0
KNEE = -66.0
COARSE = 16.0
KNEE_CODE = (KNEE - TOP) * FINE + 65535.0
VMEM_LIMIT = 48 * 1024 * 1024


def dft_tables(feeds):
    hi, big, low = np.meshgrid(np.arange(4), np.arange(feeds // 8), np.arange(2), indexing="ij")
    beam = (8 * big + 2 * hi + low).reshape(-1)
    feed = np.arange(feeds)
    angle = (beam[:, None] * feed[None, :] % feeds) * (2.0 * math.pi / feeds)
    cosine = np.cos(angle) / math.sqrt(feeds)
    sine = np.sin(angle) / math.sqrt(feeds)
    real = np.stack([cosine.reshape(feeds, -1, 8), sine.reshape(feeds, -1, 8)], axis=2)
    imag = np.stack([-sine.reshape(feeds, -1, 8), cosine.reshape(feeds, -1, 8)], axis=2)
    table = np.concatenate([real, imag], axis=0).reshape(2 * feeds, 2 * feeds)
    high = table.astype(ml_dtypes.bfloat16)
    rest = (table - high.astype(np.float64)).astype(ml_dtypes.bfloat16)
    return high, rest


def lane_index(shape):
    return lax.broadcasted_iota(jnp.int32, shape, len(shape) - 1)


def roll(x, by):
    return pltpu.roll(x, by % x.shape[-1], x.ndim - 1)


def swap_blocks(rows):
    lane = lane_index(rows[0].shape)
    low_half = lane < 64
    even = lane % 64 < 32
    mid = [None] * 4
    for n in range(2):
        mid[n] = jnp.where(low_half, rows[n], roll(rows[n + 2], 64))
        mid[n + 2] = jnp.where(low_half, roll(rows[n], 64), rows[n + 2])
    out = [None] * 4
    for n in (0, 2):
        out[n] = jnp.where(even, mid[n], roll(mid[n + 1], 32))
        out[n + 1] = jnp.where(even, roll(mid[n], -32), mid[n + 1])
    return out


def encode(x):
    level = jnp.log2(jnp.maximum(x, 2.0**-126))
    fine = (level - TOP) * FINE + 65535.0
    coarse = (level - KNEE) * COARSE + KNEE_CODE
    code = jnp.floor(jnp.maximum(fine, coarse) + 0.5).astype(jnp.int32)
    return jnp.where(x > 0.0, code, 0)


def decode(code):
    value = code.astype(jnp.float32)
    fine = (value - 65535.0) * (1.0 / FINE) + TOP
    coarse = (value - KNEE_CODE) * (1.0 / COARSE) + KNEE
    return jnp.where(code > 0, jnp.exp2(jnp.minimum(fine, coarse)), 0.0)


def pack_kernel(x_ref, out_ref):
    tiles = x_ref.shape[2] // LANES

    def step(j, _):
        lanes = pl.ds(pl.multiple_of(j * LANES, LANES), LANES)
        rows = [x_ref[n, :, lanes].astype(jnp.float32) for n in range(4)]
        for g, value in enumerate(swap_blocks(rows)):
            out_ref[4 * j + g] = value.astype(jnp.bfloat16)
        return 0

    lax.fori_loop(0, tiles, step, 0, unroll=4)


def beam_kernel(high_ref, rest_ref, x_ref, out_ref):
    sources, blocks, cf, lanes = x_ref.shape
    several = 2
    feeds = high_ref.shape[0] // 2
    rows = feeds // 4
    lane = lane_index((rows, lanes))
    even = lane % 64 < 32
    low_half = lane < 64
    for y in range(0, blocks, several):
        x = jnp.concatenate(
            [x_ref[:, y + k].reshape(sources * cf, lanes) for k in range(several)], axis=1
        )
        beam = jnp.dot(high_ref[...], x, preferred_element_type=jnp.float32)
        beam = beam + jnp.dot(rest_ref[...], x, preferred_element_type=jnp.float32)
        power = beam[:feeds] * beam[:feeds] + beam[feeds:] * beam[feeds:]
        for k in range(several):
            p = [
                power[g * rows : (g + 1) * rows, k * lanes : (k + 1) * lanes] for g in range(4)
            ]
            pairs = [
                jnp.where(even, p[g] + roll(p[g], -32), p[g + 1] + roll(p[g + 1], 32))
                for g in (0, 2)
            ]
            first = jnp.where(low_half, pairs[0], roll(pairs[1], 64))
            second = jnp.where(low_half, roll(pairs[0], 64), pairs[1])
            out_ref[2 * (y + k)] = (first * (1.0 / DS)).astype(jnp.bfloat16)
            out_ref[2 * (y + k) + 1] = (second * (1.0 / DS)).astype(jnp.bfloat16)


def tree_kernel(place_ref, core_ref, lag_ref, off_ref, own_ref, other_ref, out_ref):
    count = own_ref.shape[0]
    times = 2 * count
    rows = 8
    lane = lane_index((rows, LANES))
    channel = lane % GROUP
    place = place_ref[0]

    per_lag = LANES // GROUP
    lag = jnp.broadcast_to(lag_ref[pl.ds(place // per_lag, 1), :], (rows, LANES))
    lag = jnp.take_along_axis(lag, (place % per_lag) * GROUP + channel, axis=1)
    half_group = GROUP // 2
    per_off = LANES // half_group
    start = pl.multiple_of(place // per_off * LANES, LANES)
    uppers, takes, partners = [], [], []
    for s in range(SECTIONS):
        h = 2**s
        values = jnp.broadcast_to(off_ref[pl.ds(s, 1), pl.ds(start, LANES)], (rows, LANES))
        pair = h * (channel // (2 * h)) + channel % h
        off = jnp.take_along_axis(values, (place % per_off) * half_group + pair, axis=1)
        upper = (channel // h) % 2 == 1
        uppers.append(upper)
        takes.append(jnp.logical_and(upper, off == 1))
        partners.append(jnp.where(upper, lane - h, lane + h))

    zero = jnp.zeros((rows, LANES), jnp.float32)

    def back(level, t, by):
        return level[t - by] if t >= by else zero

    def run(is_odd):
        def step(k, _):
            at = pl.ds(pl.multiple_of(k * 2 * rows, 2 * rows), 2 * rows)
            for q in range(2):
                level = []
                for t in range(times):
                    mine = (t // 2) % 2 == (1 if is_odd else 0)
                    source = own_ref if mine else other_ref
                    block = source[t // 4 * 2 + t % 2, at, :].astype(jnp.float32)
                    level.append(block[q * rows : (q + 1) * rows])
                level = [
                    jnp.where(
                        lag == 0,
                        level[t],
                        jnp.where(lag == 1, back(level, t, 1), back(level, t, 2)),
                    )
                    for t in range(times)
                ]
                for s in range(SECTIONS):
                    after = []
                    for t in range(times):
                        mine = (t // 2) % 2 == (1 if is_odd else 0)
                        if s == SECTIONS - 1 and not mine:
                            after.append(None)
                            continue
                        one, two = back(level, t, 1), back(level, t, 2)
                        sent = jnp.where(takes[s], one, level[t])
                        kept = jnp.where(takes[s], two, jnp.where(uppers[s], one, level[t]))
                        after.append(kept + jnp.take_along_axis(sent, partners[s], axis=1))
                    level = after
                scale = 1.0 / 2**SECTIONS
                for y in range(count // 2):
                    t = 4 * y + (2 if is_odd else 0)
                    word = encode(level[t] * scale) | (encode(level[t + 1] * scale) << 16)
                    for i in range(rows // 2):
                        out_ref[(2 * k + q) * (rows // 2) + i, y] = word[2 * i : 2 * i + 2]
            return 0

        lax.fori_loop(0, own_ref.shape[1] // (2 * rows), step, 0)

    @pl.when(core_ref[0] == 0)
    def _():
        run(False)

    @pl.when(core_ref[0] != 0)
    def _():
        run(True)


def unpack_kernel(x_ref, out_ref):
    tiles = x_ref.shape[0]
    lane = lane_index((8, LANES))
    row = lax.broadcasted_iota(jnp.int32, (8, LANES), 0)
    stay_far = (row < 4) == (lane < 64)
    low_row = row % 4 < 2
    stay_near = low_row == (lane % 64 < 32)

    def step(j, _):
        v = x_ref[j]
        u = jnp.where(stay_far, v, roll(pltpu.roll(v, 4, 0), 64))
        moved = jnp.where(
            low_row, roll(pltpu.roll(u, 6, 0), 32), roll(pltpu.roll(u, 2, 0), -32)
        )
        w = jnp.where(stay_near, u, moved)
        lanes = pl.ds(pl.multiple_of(j * LANES, LANES), LANES)
        out_ref[0, :, lanes] = decode(w & 65535)
        out_ref[1, :, lanes] = decode((w >> 16) & 65535)
        return 0

    lax.fori_loop(0, tiles, step, 0, unroll=4)


def on_device(high, rest, voltages, channel_lag, offsets):
    parts, local, samp, channels = voltages.shape
    feed_count = lax.axis_size("feed")
    y_count = lax.axis_size("y")
    peers = feed_count * y_count
    cf = parts * local
    params = pltpu.CompilerParams(vmem_limit_bytes=VMEM_LIMIT)
    vmem = pl.BlockSpec(memory_space=pltpu.VMEM)
    smem = pl.BlockSpec(memory_space=pltpu.SMEM)

    def call(kernel, name, shape, dtype, specs, *operands):
        return pl.pallas_call(
            kernel,
            in_specs=specs,
            out_specs=vmem,
            out_shape=jax.ShapeDtypeStruct(shape, dtype),
            compiler_params=params,
            name=name,
        )(*operands)

    rows = voltages.reshape(cf, samp, channels).transpose(1, 0, 2)
    packed = call(pack_kernel, "pack", (peers, cf, LANES), jnp.bfloat16, [vmem], rows)
    turned = lax.all_to_all(packed, ("feed", "y"), split_axis=0, concat_axis=0, tiled=True)
    turned = turned.reshape(feed_count, y_count, cf, LANES)
    beams = feed_count * local
    own = call(
        beam_kernel,
        "beams",
        (2 * y_count, beams // 4, LANES),
        jnp.bfloat16,
        [vmem] * 3,
        high,
        rest,
        turned,
    )
    other = lax.ppermute(own, "core", [(0, 1), (1, 0)])
    place = (lax.axis_index("feed") * y_count + lax.axis_index("y")).reshape(1)
    core = lax.axis_index("core").reshape(1)
    codes = call(
        tree_kernel,
        "tree",
        (feed_count, y_count, 2, LANES),
        jnp.int32,
        [smem, smem] + [vmem] * 4,
        place,
        core,
        channel_lag.reshape(-1, LANES),
        offsets,
        own,
        other,
    ).reshape(peers, 2, LANES)
    back = lax.all_to_all(codes, ("feed", "y"), split_axis=0, concat_axis=0, tiled=True)
    out = call(
        unpack_kernel,
        "unpack",
        (2, 8, channels),
        jnp.float32,
        [vmem],
        back.reshape(peers // 4, 8, LANES),
    )
    return out.transpose(1, 0, 2)


def solution(mesh):
    devices = mesh.devices
    fine = Mesh(devices.reshape(devices.shape[0], -1, 2), ("feed", "y", "core"))
    high, rest = dft_tables(8 * devices.shape[0])
    times = ("y", "core")
    body = jax.shard_map(
        functools.partial(on_device),
        mesh=fine,
        in_specs=(P(), P(), P(None, "feed", times, None), P(), P()),
        out_specs=P("feed", times, None),
        check_vma=False,
    )

    def run(voltages, channel_lag, offsets):
        return body(jnp.asarray(high), jnp.asarray(rest), voltages, channel_lag, offsets)

    return run
```

```python
import functools
import math

import jax
import jax.numpy as jnp
import ml_dtypes
import numpy as np
from jax import lax
from jax.experimental import pallas as pl
from jax.experimental.pallas import tpu as pltpu
from jax.sharding import Mesh
from jax.sharding import PartitionSpec as P

DS = 2
SECTIONS = 5
GROUP = 2**SECTIONS
LANES = 128
TOP = 14.5
FINE = 800.0
KNEE = -66.0
COARSE = 16.0
KNEE_CODE = (KNEE - TOP) * FINE + 65535.0
VMEM_LIMIT = 48 * 1024 * 1024


def dft_tables(feeds):
    hi, big, low = np.meshgrid(np.arange(4), np.arange(feeds // 8), np.arange(2), indexing="ij")
    beam = (8 * big + 2 * hi + low).reshape(-1)
    feed = np.arange(feeds)
    angle = (beam[:, None] * feed[None, :] % feeds) * (2.0 * math.pi / feeds)
    cosine = np.cos(angle) / math.sqrt(feeds)
    sine = np.sin(angle) / math.sqrt(feeds)
    real = np.stack([cosine.reshape(feeds, -1, 8), sine.reshape(feeds, -1, 8)], axis=2)
    imag = np.stack([-sine.reshape(feeds, -1, 8), cosine.reshape(feeds, -1, 8)], axis=2)
    table = np.concatenate([real, imag], axis=0).reshape(2 * feeds, 2 * feeds)
    high = table.astype(ml_dtypes.bfloat16)
    rest = (table - high.astype(np.float64)).astype(ml_dtypes.bfloat16)
    return high, rest


def lane_index(shape):
    return lax.broadcasted_iota(jnp.int32, shape, len(shape) - 1)


def roll(x, by):
    return pltpu.roll(x, by % x.shape[-1], x.ndim - 1)


def swap_blocks(rows):
    lane = lane_index(rows[0].shape)
    low_half = lane < 64
    even = lane % 64 < 32
    turned = [rows[0]] + [roll(rows[n], 32 * n) for n in range(1, 4)]
    out = []
    for g in range(4):
        blocks = [turned[(m - g) % 4] for m in range(4)]
        mixed = jnp.where(
            low_half,
            jnp.where(even, blocks[0], blocks[1]),
            jnp.where(even, blocks[2], blocks[3]),
        )
        out.append(roll(mixed, -32 * g) if g else mixed)
    return out


def encode(x):
    level = jnp.log2(jnp.maximum(x, 2.0**-126))
    fine = (level - TOP) * FINE + 65535.0
    coarse = (level - KNEE) * COARSE + KNEE_CODE
    code = jnp.floor(jnp.maximum(fine, coarse) + 0.5).astype(jnp.int32)
    return jnp.where(x > 0.0, code, 0)


def decode(code):
    value = code.astype(jnp.float32)
    fine = (value - 65535.0) * (1.0 / FINE) + TOP
    coarse = (value - KNEE_CODE) * (1.0 / COARSE) + KNEE
    return jnp.where(code > 0, jnp.exp2(jnp.minimum(fine, coarse)), 0.0)


def pack_kernel(x_ref, out_ref):
    tiles = x_ref.shape[2] // LANES

    def step(j, _):
        lanes = pl.ds(pl.multiple_of(j * LANES, LANES), LANES)
        rows = [x_ref[n, :, lanes] for n in range(4)]
        for g, value in enumerate(swap_blocks(rows)):
            out_ref[4 * j + g] = value
        return 0

    lax.fori_loop(0, tiles, step, 0, unroll=16)


def beam_kernel(high_ref, rest_ref, x_ref, out_ref):
    sources, blocks, cf, lanes = x_ref.shape
    several = 2
    feeds = high_ref.shape[0] // 2
    rows = feeds // 4
    lane = lane_index((rows, lanes))
    even = lane % 64 < 32
    low_half = lane < 64
    for y in range(0, blocks, several):
        x = jnp.concatenate(
            [x_ref[:, y + k].reshape(sources * cf, lanes) for k in range(several)], axis=1
        )
        beam = jnp.dot(high_ref[...], x, preferred_element_type=jnp.float32)
        beam = beam + jnp.dot(rest_ref[...], x, preferred_element_type=jnp.float32)
        power = beam[:feeds] * beam[:feeds] + beam[feeds:] * beam[feeds:]
        for k in range(several):
            p = [
                power[g * rows : (g + 1) * rows, k * lanes : (k + 1) * lanes] for g in range(4)
            ]
            pairs = [
                jnp.where(even, p[g] + roll(p[g], -32), p[g + 1] + roll(p[g + 1], 32))
                for g in (0, 2)
            ]
            first = jnp.where(low_half, pairs[0], roll(pairs[1], 64))
            second = jnp.where(low_half, roll(pairs[0], 64), pairs[1])
            out_ref[2 * (y + k)] = (first * (1.0 / DS)).astype(jnp.bfloat16)
            out_ref[2 * (y + k) + 1] = (second * (1.0 / DS)).astype(jnp.bfloat16)


def tree_kernel(place_ref, core_ref, lag_ref, off_ref, own_ref, other_ref, out_ref):
    count = own_ref.shape[0]
    times = 2 * count
    rows = 8
    lane = lane_index((rows, LANES))
    channel = lane % GROUP
    place = place_ref[0]

    per_lag = LANES // GROUP
    lag = jnp.broadcast_to(lag_ref[pl.ds(place // per_lag, 1), :], (rows, LANES))
    lag = jnp.take_along_axis(lag, (place % per_lag) * GROUP + channel, axis=1)
    half_group = GROUP // 2
    per_off = LANES // half_group
    start = pl.multiple_of(place // per_off * LANES, LANES)
    uppers, takes, partners = [], [], []
    for s in range(SECTIONS):
        h = 2**s
        values = jnp.broadcast_to(off_ref[pl.ds(s, 1), pl.ds(start, LANES)], (rows, LANES))
        pair = h * (channel // (2 * h)) + channel % h
        off = jnp.take_along_axis(values, (place % per_off) * half_group + pair, axis=1)
        upper = (channel // h) % 2 == 1
        uppers.append(upper)
        takes.append(jnp.logical_and(upper, off == 1))
        partners.append(jnp.where(upper, lane - h, lane + h))

    zero = jnp.zeros((rows, LANES), jnp.float32)

    def back(level, t, by):
        return level[t - by] if t >= by else zero

    def run(is_odd):
        def step(k, _):
            at = pl.ds(pl.multiple_of(k * 2 * rows, 2 * rows), 2 * rows)
            for q in range(2):
                level = []
                for t in range(times):
                    mine = (t // 2) % 2 == (1 if is_odd else 0)
                    source = own_ref if mine else other_ref
                    block = source[t // 4 * 2 + t % 2, at, :].astype(jnp.float32)
                    level.append(block[q * rows : (q + 1) * rows])
                level = [
                    jnp.where(
                        lag == 0,
                        level[t],
                        jnp.where(lag == 1, back(level, t, 1), back(level, t, 2)),
                    )
                    for t in range(times)
                ]
                for s in range(SECTIONS):
                    after = []
                    for t in range(times):
                        mine = (t // 2) % 2 == (1 if is_odd else 0)
                        if s == SECTIONS - 1 and not mine:
                            after.append(None)
                            continue
                        one, two = back(level, t, 1), back(level, t, 2)
                        sent = jnp.where(takes[s], one, level[t])
                        kept = jnp.where(takes[s], two, jnp.where(uppers[s], one, level[t]))
                        after.append(kept + jnp.take_along_axis(sent, partners[s], axis=1))
                    level = after
                scale = 1.0 / 2**SECTIONS
                for y in range(count // 2):
                    t = 4 * y + (2 if is_odd else 0)
                    word = encode(level[t] * scale) | (encode(level[t + 1] * scale) << 16)
                    for i in range(rows // 2):
                        out_ref[(2 * k + q) * (rows // 2) + i, y] = word[2 * i : 2 * i + 2]
            return 0

        lax.fori_loop(0, own_ref.shape[1] // (2 * rows), step, 0)

    @pl.when(core_ref[0] == 0)
    def _():
        run(False)

    @pl.when(core_ref[0] != 0)
    def _():
        run(True)


def unpack_kernel(x_ref, out_ref):
    tiles = x_ref.shape[0]
    lane = lane_index((8, LANES))
    row = lax.broadcasted_iota(jnp.int32, (8, LANES), 0)
    stay_far = (row < 4) == (lane < 64)
    low_row = row % 4 < 2
    stay_near = low_row == (lane % 64 < 32)

    def step(j, _):
        v = x_ref[j]
        u = jnp.where(stay_far, v, roll(pltpu.roll(v, 4, 0), 64))
        moved = jnp.where(
            low_row, roll(pltpu.roll(u, 6, 0), 32), roll(pltpu.roll(u, 2, 0), -32)
        )
        w = jnp.where(stay_near, u, moved)
        lanes = pl.ds(pl.multiple_of(j * LANES, LANES), LANES)
        for k in range(2):
            twice = jnp.take_along_axis(w, row // 2 + 4 * k, axis=0)
            value = decode(jnp.where(row % 2 == 1, twice >> 16, twice) & 65535)
            out_ref[4 * k : 4 * k + 4, :, lanes] = value.reshape(4, 2, LANES)
        return 0

    lax.fori_loop(0, tiles, step, 0, unroll=16)


def on_device(high, rest, voltages, channel_lag, offsets):
    parts, local, samp, channels = voltages.shape
    feed_count = lax.axis_size("feed")
    y_count = lax.axis_size("y")
    peers = feed_count * y_count
    cf = parts * local
    params = pltpu.CompilerParams(vmem_limit_bytes=VMEM_LIMIT)
    vmem = pl.BlockSpec(memory_space=pltpu.VMEM)
    smem = pl.BlockSpec(memory_space=pltpu.SMEM)

    def call(kernel, name, shape, dtype, specs, *operands):
        return pl.pallas_call(
            kernel,
            in_specs=specs,
            out_specs=vmem,
            out_shape=jax.ShapeDtypeStruct(shape, dtype),
            compiler_params=params,
            name=name,
        )(*operands)

    rows = voltages.reshape(cf, samp, channels).transpose(1, 0, 2)
    packed = call(pack_kernel, "pack", (peers, cf, LANES), jnp.bfloat16, [vmem], rows)
    turned = lax.all_to_all(packed, ("feed", "y"), split_axis=0, concat_axis=0, tiled=True)
    turned = turned.reshape(feed_count, y_count, cf, LANES)
    beams = feed_count * local
    own = call(
        beam_kernel,
        "beams",
        (2 * y_count, beams // 4, LANES),
        jnp.bfloat16,
        [vmem] * 3,
        high,
        rest,
        turned,
    )
    other = lax.ppermute(own, "core", [(0, 1), (1, 0)])
    place = (lax.axis_index("feed") * y_count + lax.axis_index("y")).reshape(1)
    core = lax.axis_index("core").reshape(1)
    codes = call(
        tree_kernel,
        "tree",
        (feed_count, y_count, 2, LANES),
        jnp.int32,
        [smem, smem] + [vmem] * 4,
        place,
        core,
        channel_lag.reshape(-1, LANES),
        offsets,
        own,
        other,
    ).reshape(peers, 2, LANES)
    back = lax.all_to_all(codes, ("feed", "y"), split_axis=0, concat_axis=0, tiled=True)
    return call(
        unpack_kernel,
        "unpack",
        (8, 2, channels),
        jnp.float32,
        [vmem],
        back.reshape(peers // 4, 8, LANES),
    )


def solution(mesh):
    devices = mesh.devices
    fine = Mesh(devices.reshape(devices.shape[0], -1, 2), ("feed", "y", "core"))
    high, rest = dft_tables(8 * devices.shape[0])
    times = ("y", "core")
    body = jax.shard_map(
        functools.partial(on_device),
        mesh=fine,
        in_specs=(P(), P(), P(None, "feed", times, None), P(), P()),
        out_specs=P("feed", times, None),
        check_vma=False,
    )

    def run(voltages, channel_lag, offsets):
        return body(jnp.asarray(high), jnp.asarray(rest), voltages, channel_lag, offsets)

    return run
```

```python
import functools
import math

import jax
import jax.numpy as jnp
import ml_dtypes
import numpy as np
from jax import lax
from jax.experimental import pallas as pl
from jax.experimental.pallas import tpu as pltpu
from jax.sharding import Mesh
from jax.sharding import PartitionSpec as P

DS = 2
SECTIONS = 5
GROUP = 2**SECTIONS
LANES = 128
TOP = 14.5
FINE = 800.0
KNEE = -66.0
COARSE = 16.0
KNEE_CODE = (KNEE - TOP) * FINE + 65535.0
VMEM_LIMIT = 48 * 1024 * 1024


def dft_tables(feeds):
    hi, big, low = np.meshgrid(np.arange(4), np.arange(feeds // 8), np.arange(2), indexing="ij")
    beam = (8 * big + 2 * hi + low).reshape(-1)
    feed = np.arange(feeds)
    angle = (beam[:, None] * feed[None, :] % feeds) * (2.0 * math.pi / feeds)
    cosine = np.cos(angle) / math.sqrt(feeds)
    sine = np.sin(angle) / math.sqrt(feeds)
    real = np.stack([cosine.reshape(feeds, -1, 8), sine.reshape(feeds, -1, 8)], axis=2)
    imag = np.stack([-sine.reshape(feeds, -1, 8), cosine.reshape(feeds, -1, 8)], axis=2)
    table = np.concatenate([real, imag], axis=0).reshape(2 * feeds, 2 * feeds)
    high = table.astype(ml_dtypes.bfloat16)
    rest = (table - high.astype(np.float64)).astype(ml_dtypes.bfloat16)
    return high, rest


def lane_index(shape):
    return lax.broadcasted_iota(jnp.int32, shape, len(shape) - 1)


def roll(x, by):
    return pltpu.roll(x, by % x.shape[-1], x.ndim - 1)


def swap_blocks(rows):
    lane = lane_index(rows[0].shape)
    low_half = lane < 64
    even = lane % 64 < 32
    turned = [rows[0]] + [roll(rows[n], 32 * n) for n in range(1, 4)]
    out = []
    for g in range(4):
        blocks = [turned[(m - g) % 4] for m in range(4)]
        mixed = jnp.where(
            low_half,
            jnp.where(even, blocks[0], blocks[1]),
            jnp.where(even, blocks[2], blocks[3]),
        )
        out.append(roll(mixed, -32 * g) if g else mixed)
    return out


def encode(x):
    level = jnp.log2(jnp.maximum(x, 2.0**-126))
    fine = (level - TOP) * FINE + 65535.0
    coarse = (level - KNEE) * COARSE + KNEE_CODE
    code = jnp.floor(jnp.maximum(fine, coarse) + 0.5).astype(jnp.int32)
    return jnp.where(x > 0.0, code, 0)


def decode(code):
    value = code.astype(jnp.float32)
    fine = (value - 65535.0) * (1.0 / FINE) + TOP
    coarse = (value - KNEE_CODE) * (1.0 / COARSE) + KNEE
    return jnp.where(code > 0, jnp.exp2(jnp.minimum(fine, coarse)), 0.0)


def pack_kernel(x_ref, out_ref):
    tiles = x_ref.shape[2] // LANES

    def step(j, _):
        lanes = pl.ds(pl.multiple_of(j * LANES, LANES), LANES)
        rows = [x_ref[n, :, lanes] for n in range(4)]
        for g, value in enumerate(swap_blocks(rows)):
            out_ref[4 * j + g] = value
        return 0

    lax.fori_loop(0, tiles, step, 0, unroll=16)


def beam_kernel(high_ref, rest_ref, x_ref, out_ref):
    sources, blocks, cf, lanes = x_ref.shape
    several = 2
    feeds = high_ref.shape[0] // 2
    rows = feeds // 4
    lane = lane_index((rows, lanes))
    even = lane % 64 < 32
    low_half = lane < 64
    for y in range(0, blocks, several):
        x = jnp.concatenate(
            [x_ref[:, y + k].reshape(sources * cf, lanes) for k in range(several)], axis=1
        )
        beam = jnp.dot(high_ref[...], x, preferred_element_type=jnp.float32)
        beam = beam + jnp.dot(rest_ref[...], x, preferred_element_type=jnp.float32)
        power = beam[:feeds] * beam[:feeds] + beam[feeds:] * beam[feeds:]
        for k in range(several):
            p = [
                power[g * rows : (g + 1) * rows, k * lanes : (k + 1) * lanes] for g in range(4)
            ]
            pairs = [
                jnp.where(even, p[g] + roll(p[g], -32), p[g + 1] + roll(p[g + 1], 32))
                for g in (0, 2)
            ]
            first = jnp.where(low_half, pairs[0], roll(pairs[1], 64))
            second = jnp.where(low_half, roll(pairs[0], 64), pairs[1])
            out_ref[2 * (y + k)] = (first * (1.0 / DS)).astype(jnp.bfloat16)
            out_ref[2 * (y + k) + 1] = (second * (1.0 / DS)).astype(jnp.bfloat16)


def tree_kernel(place_ref, core_ref, lag_ref, off_ref, own_ref, other_ref, out_ref):
    count = own_ref.shape[0]
    times = 2 * count
    rows = 8
    lane = lane_index((rows, LANES))
    channel = lane % GROUP
    place = place_ref[0]

    per_lag = LANES // GROUP
    lag = jnp.broadcast_to(lag_ref[pl.ds(place // per_lag, 1), :], (rows, LANES))
    lag = jnp.take_along_axis(lag, (place % per_lag) * GROUP + channel, axis=1)
    half_group = GROUP // 2
    per_off = LANES // half_group
    start = pl.multiple_of(place // per_off * LANES, LANES)
    uppers, takes, partners = [], [], []
    for s in range(SECTIONS):
        h = 2**s
        values = jnp.broadcast_to(off_ref[pl.ds(s, 1), pl.ds(start, LANES)], (rows, LANES))
        pair = h * (channel // (2 * h)) + channel % h
        off = jnp.take_along_axis(values, (place % per_off) * half_group + pair, axis=1)
        upper = (channel // h) % 2 == 1
        uppers.append(upper)
        takes.append(jnp.logical_and(upper, off == 1))
        partners.append(jnp.where(upper, lane - h, lane + h))

    zero = jnp.zeros((rows, LANES), jnp.float32)

    def back(level, t, by):
        return level[t - by] if t >= by else zero

    def run(is_odd):
        def step(k, _):
            at = pl.ds(pl.multiple_of(k * 2 * rows, 2 * rows), 2 * rows)
            for q in range(2):
                level = []
                for t in range(times):
                    mine = (t // 2) % 2 == (1 if is_odd else 0)
                    source = own_ref if mine else other_ref
                    block = source[t // 4 * 2 + t % 2, at, :].astype(jnp.float32)
                    level.append(block[q * rows : (q + 1) * rows])
                level = [
                    jnp.where(
                        lag == 0,
                        level[t],
                        jnp.where(lag == 1, back(level, t, 1), back(level, t, 2)),
                    )
                    for t in range(times)
                ]
                for s in range(SECTIONS):
                    after = []
                    for t in range(times):
                        mine = (t // 2) % 2 == (1 if is_odd else 0)
                        if s == SECTIONS - 1 and not mine:
                            after.append(None)
                            continue
                        one, two = back(level, t, 1), back(level, t, 2)
                        sent = jnp.where(takes[s], one, level[t])
                        kept = jnp.where(takes[s], two, jnp.where(uppers[s], one, level[t]))
                        after.append(kept + jnp.take_along_axis(sent, partners[s], axis=1))
                    level = after
                scale = 1.0 / 2**SECTIONS
                for y in range(count // 2):
                    t = 4 * y + (2 if is_odd else 0)
                    word = encode(level[t] * scale) | (encode(level[t + 1] * scale) << 16)
                    for i in range(rows // 2):
                        out_ref[(2 * k + q) * (rows // 2) + i, y] = word[2 * i : 2 * i + 2]
            return 0

        lax.fori_loop(0, own_ref.shape[1] // (2 * rows), step, 0)

    @pl.when(core_ref[0] == 0)
    def _():
        run(False)

    @pl.when(core_ref[0] != 0)
    def _():
        run(True)


def unpack_kernel(x_ref, out_ref):
    tiles = x_ref.shape[0]
    lane = lane_index((8, LANES))
    row = lax.broadcasted_iota(jnp.int32, (8, LANES), 0)
    stay_far = (row < 4) == (lane < 64)
    low_row = row % 4 < 2
    stay_near = low_row == (lane % 64 < 32)

    def step(j, _):
        v = x_ref[j]
        u = jnp.where(stay_far, v, roll(pltpu.roll(v, 4, 0), 64))
        moved = jnp.where(
            low_row, roll(pltpu.roll(u, 6, 0), 32), roll(pltpu.roll(u, 2, 0), -32)
        )
        w = jnp.where(stay_near, u, moved)
        lanes = pl.ds(pl.multiple_of(j * LANES, LANES), LANES)
        for k in range(2):
            twice = jnp.take_along_axis(w, row // 2 + 4 * k, axis=0)
            value = decode(jnp.where(row % 2 == 1, twice >> 16, twice) & 65535)
            out_ref[4 * k : 4 * k + 4, :, lanes] = value.reshape(4, 2, LANES)
        return 0

    lax.fori_loop(0, tiles, step, 0, unroll=16)


def on_device(high, rest, voltages, channel_lag, offsets):
    parts, local, samp, channels = voltages.shape
    feed_count = lax.axis_size("feed")
    y_count = lax.axis_size("y")
    peers = feed_count * y_count
    cf = parts * local
    params = pltpu.CompilerParams(vmem_limit_bytes=VMEM_LIMIT)
    vmem = pl.BlockSpec(memory_space=pltpu.VMEM)
    smem = pl.BlockSpec(memory_space=pltpu.SMEM)

    def call(kernel, name, shape, dtype, specs, *operands):
        return pl.pallas_call(
            kernel,
            in_specs=specs,
            out_specs=vmem,
            out_shape=jax.ShapeDtypeStruct(shape, dtype),
            compiler_params=params,
            name=name,
        )(*operands)

    rows = voltages.reshape(cf, samp, channels).transpose(1, 0, 2)
    packed = call(pack_kernel, "pack", (peers, cf, LANES), jnp.bfloat16, [vmem], rows)
    turned = lax.all_to_all(packed, "feed", split_axis=0, concat_axis=0, tiled=True)
    turned = turned.reshape(feed_count, y_count, cf, LANES)
    beams = feed_count * local
    own = call(
        beam_kernel,
        "beams",
        (2 * y_count, beams // 4, LANES),
        jnp.bfloat16,
        [vmem] * 3,
        high,
        rest,
        turned,
    )
    own = lax.all_to_all(own, "y", split_axis=0, concat_axis=0, tiled=True)
    other = lax.ppermute(own, "core", [(0, 1), (1, 0)])
    place = (lax.axis_index("feed") * y_count + lax.axis_index("y")).reshape(1)
    core = lax.axis_index("core").reshape(1)
    codes = call(
        tree_kernel,
        "tree",
        (feed_count, y_count, 2, LANES),
        jnp.int32,
        [smem, smem] + [vmem] * 4,
        place,
        core,
        channel_lag.reshape(-1, LANES),
        offsets,
        own,
        other,
    ).reshape(peers, 2, LANES)
    back = lax.all_to_all(codes, ("feed", "y"), split_axis=0, concat_axis=0, tiled=True)
    return call(
        unpack_kernel,
        "unpack",
        (8, 2, channels),
        jnp.float32,
        [vmem],
        back.reshape(peers // 4, 8, LANES),
    )


def solution(mesh):
    devices = mesh.devices
    fine = Mesh(devices.reshape(devices.shape[0], -1, 2), ("feed", "y", "core"))
    high, rest = dft_tables(8 * devices.shape[0])
    times = ("y", "core")
    body = jax.shard_map(
        functools.partial(on_device),
        mesh=fine,
        in_specs=(P(), P(), P(None, "feed", times, None), P(), P()),
        out_specs=P("feed", times, None),
        check_vma=False,
    )

    def run(voltages, channel_lag, offsets):
        return body(jnp.asarray(high), jnp.asarray(rest), voltages, channel_lag, offsets)

    return run
```

```python
import functools
import math

import jax
import jax.numpy as jnp
import ml_dtypes
import numpy as np
from jax import lax
from jax.experimental import pallas as pl
from jax.experimental.pallas import tpu as pltpu
from jax.sharding import Mesh
from jax.sharding import PartitionSpec as P

DS = 2
SECTIONS = 5
GROUP = 2**SECTIONS
LANES = 128
TOP = 14.5
FINE = 800.0
KNEE = -66.0
COARSE = 16.0
KNEE_CODE = (KNEE - TOP) * FINE + 65535.0
LEAST = -126.0
LEAST_CODE = int((LEAST - KNEE) * COARSE + KNEE_CODE)
VMEM_LIMIT = 48 * 1024 * 1024


def dft_tables(feeds):
    hi, big, low = np.meshgrid(np.arange(4), np.arange(feeds // 8), np.arange(2), indexing="ij")
    beam = (8 * big + 2 * hi + low).reshape(-1)
    feed = np.arange(feeds)
    angle = (beam[:, None] * feed[None, :] % feeds) * (2.0 * math.pi / feeds)
    cosine = np.cos(angle) / math.sqrt(feeds)
    sine = np.sin(angle) / math.sqrt(feeds)
    real = np.stack([cosine.reshape(feeds, -1, 8), sine.reshape(feeds, -1, 8)], axis=2)
    imag = np.stack([-sine.reshape(feeds, -1, 8), cosine.reshape(feeds, -1, 8)], axis=2)
    table = np.concatenate([real, imag], axis=0).reshape(2 * feeds, 2 * feeds)
    high = table.astype(ml_dtypes.bfloat16)
    rest = (table - high.astype(np.float64)).astype(ml_dtypes.bfloat16)
    return high, rest


def lane_index(shape):
    return lax.broadcasted_iota(jnp.int32, shape, len(shape) - 1)


def roll(x, by):
    return pltpu.roll(x, by % x.shape[-1], x.ndim - 1)


def swap_blocks(rows):
    lane = lane_index(rows[0].shape)
    low_half = lane < 64
    even = lane % 64 < 32
    turned = [rows[0]] + [roll(rows[n], 32 * n) for n in range(1, 4)]
    out = []
    for g in range(4):
        blocks = [turned[(m - g) % 4] for m in range(4)]
        mixed = jnp.where(
            low_half,
            jnp.where(even, blocks[0], blocks[1]),
            jnp.where(even, blocks[2], blocks[3]),
        )
        out.append(roll(mixed, -32 * g) if g else mixed)
    return out


def encode(x):
    level = jnp.log2(jnp.maximum(x, 2.0**LEAST))
    fine = level * FINE + (65535.5 - TOP * FINE)
    coarse = level * COARSE + (KNEE_CODE + 0.5 - KNEE * COARSE)
    return jnp.maximum(fine, coarse).astype(jnp.int32)


def decode(code):
    value = code.astype(jnp.float32)
    fine = value * (1.0 / FINE) + (TOP - 65535.0 / FINE)
    coarse = value * (1.0 / COARSE) + (KNEE - KNEE_CODE / COARSE)
    return jnp.where(code > LEAST_CODE, jnp.exp2(jnp.minimum(fine, coarse)), 0.0)


def pack_kernel(x_ref, out_ref):
    tiles = x_ref.shape[2] // LANES

    def step(j, _):
        lanes = pl.ds(pl.multiple_of(j * LANES, LANES), LANES)
        rows = [x_ref[n, :, lanes] for n in range(4)]
        for g, value in enumerate(swap_blocks(rows)):
            out_ref[4 * j + g] = value
        return 0

    lax.fori_loop(0, tiles, step, 0, unroll=16)


def beam_kernel(high_ref, rest_ref, x_ref, out_ref):
    sources, blocks, cf, lanes = x_ref.shape
    several = 2
    feeds = high_ref.shape[0] // 2
    rows = feeds // 4
    lane = lane_index((rows, lanes))
    even = lane % 64 < 32
    low_half = lane < 64
    for y in range(0, blocks, several):
        x = jnp.concatenate(
            [x_ref[:, y + k].reshape(sources * cf, lanes) for k in range(several)], axis=1
        )
        beam = jnp.dot(high_ref[...], x, preferred_element_type=jnp.float32)
        beam = beam + jnp.dot(rest_ref[...], x, preferred_element_type=jnp.float32)
        power = beam[:feeds] * beam[:feeds] + beam[feeds:] * beam[feeds:]
        for k in range(several):
            p = [
                power[g * rows : (g + 1) * rows, k * lanes : (k + 1) * lanes] for g in range(4)
            ]
            pairs = [
                jnp.where(even, p[g] + roll(p[g], -32), p[g + 1] + roll(p[g + 1], 32))
                for g in (0, 2)
            ]
            first = jnp.where(low_half, pairs[0], roll(pairs[1], 64))
            second = jnp.where(low_half, roll(pairs[0], 64), pairs[1])
            out_ref[2 * (y + k)] = (first * (1.0 / DS)).astype(jnp.bfloat16)
            out_ref[2 * (y + k) + 1] = (second * (1.0 / DS)).astype(jnp.bfloat16)


def tree_kernel(place_ref, core_ref, lag_ref, off_ref, own_ref, other_ref, out_ref):
    count = own_ref.shape[0]
    times = 2 * count
    rows = 8
    lane = lane_index((rows, LANES))
    channel = lane % GROUP
    place = place_ref[0]

    per_lag = LANES // GROUP
    lag = jnp.broadcast_to(lag_ref[pl.ds(place // per_lag, 1), :], (rows, LANES))
    lag = jnp.take_along_axis(lag, (place % per_lag) * GROUP + channel, axis=1)
    half_group = GROUP // 2
    per_off = LANES // half_group
    start = pl.multiple_of(place // per_off * LANES, LANES)
    uppers, takes, partners = [], [], []
    for s in range(SECTIONS):
        h = 2**s
        values = jnp.broadcast_to(off_ref[pl.ds(s, 1), pl.ds(start, LANES)], (rows, LANES))
        pair = h * (channel // (2 * h)) + channel % h
        off = jnp.take_along_axis(values, (place % per_off) * half_group + pair, axis=1)
        upper = (channel // h) % 2 == 1
        uppers.append(upper)
        takes.append(jnp.logical_and(upper, off == 1))
        partners.append(jnp.where(upper, lane - h, lane + h))

    zero = jnp.zeros((rows, LANES), jnp.float32)

    def delay(level, late):
        return [
            jnp.where(late, level[t - 1] if t else zero, level[t]) for t in range(times)
        ]

    def run(is_odd):
        def step(k, _):
            at = pl.ds(pl.multiple_of(k * 2 * rows, 2 * rows), 2 * rows)
            for q in range(2):
                level = []
                for t in range(times):
                    mine = (t // 2) % 2 == (1 if is_odd else 0)
                    source = own_ref if mine else other_ref
                    block = source[t // 4 * 2 + t % 2, at, :].astype(jnp.float32)
                    level.append(block[q * rows : (q + 1) * rows])
                level = delay(delay(level, lag >= 1), lag >= 2)
                for s in range(SECTIONS):
                    sent = delay(level, takes[s])
                    after = []
                    for t in range(times):
                        mine = (t // 2) % 2 == (1 if is_odd else 0)
                        if s == SECTIONS - 1 and not mine:
                            after.append(None)
                            continue
                        kept = jnp.where(uppers[s], sent[t - 1] if t else zero, level[t])
                        after.append(kept + jnp.take_along_axis(sent[t], partners[s], axis=1))
                    level = after
                scale = 1.0 / 2**SECTIONS
                for y in range(count // 2):
                    t = 4 * y + (2 if is_odd else 0)
                    word = encode(level[t] * scale) | (encode(level[t + 1] * scale) << 16)
                    for i in range(rows // 2):
                        out_ref[(2 * k + q) * (rows // 2) + i, y] = word[2 * i : 2 * i + 2]
            return 0

        lax.fori_loop(0, own_ref.shape[1] // (2 * rows), step, 0)

    @pl.when(core_ref[0] == 0)
    def _():
        run(False)

    @pl.when(core_ref[0] != 0)
    def _():
        run(True)


def unpack_kernel(x_ref, out_ref):
    tiles = x_ref.shape[0]
    lane = lane_index((8, LANES))
    row = lax.broadcasted_iota(jnp.int32, (8, LANES), 0)
    stay_far = (row < 4) == (lane < 64)
    low_row = row % 4 < 2
    stay_near = low_row == (lane % 64 < 32)

    def step(j, _):
        v = x_ref[j]
        u = jnp.where(stay_far, v, roll(pltpu.roll(v, 4, 0), 64))
        moved = jnp.where(
            low_row, roll(pltpu.roll(u, 6, 0), 32), roll(pltpu.roll(u, 2, 0), -32)
        )
        w = jnp.where(stay_near, u, moved)
        lanes = pl.ds(pl.multiple_of(j * LANES, LANES), LANES)
        for k in range(2):
            twice = jnp.take_along_axis(w, row // 2 + 4 * k, axis=0)
            value = decode(jnp.where(row % 2 == 1, twice >> 16, twice) & 65535)
            out_ref[4 * k : 4 * k + 4, :, lanes] = value.reshape(4, 2, LANES)
        return 0

    lax.fori_loop(0, tiles, step, 0, unroll=32)


def on_device(high, rest, voltages, channel_lag, offsets):
    parts, local, samp, channels = voltages.shape
    feed_count = lax.axis_size("feed")
    y_count = lax.axis_size("y")
    peers = feed_count * y_count
    cf = parts * local
    params = pltpu.CompilerParams(vmem_limit_bytes=VMEM_LIMIT)
    vmem = pl.BlockSpec(memory_space=pltpu.VMEM)
    smem = pl.BlockSpec(memory_space=pltpu.SMEM)

    def call(kernel, name, shape, dtype, specs, *operands):
        return pl.pallas_call(
            kernel,
            in_specs=specs,
            out_specs=vmem,
            out_shape=jax.ShapeDtypeStruct(shape, dtype),
            compiler_params=params,
            name=name,
        )(*operands)

    rows = voltages.reshape(cf, samp, channels).transpose(1, 0, 2)
    packed = call(pack_kernel, "pack", (peers, cf, LANES), jnp.bfloat16, [vmem], rows)
    turned = lax.all_to_all(packed, ("feed", "y"), split_axis=0, concat_axis=0, tiled=True)
    turned = turned.reshape(feed_count, y_count, cf, LANES)
    beams = feed_count * local
    own = call(
        beam_kernel,
        "beams",
        (2 * y_count, beams // 4, LANES),
        jnp.bfloat16,
        [vmem] * 3,
        high,
        rest,
        turned,
    )
    other = lax.ppermute(own, "core", [(0, 1), (1, 0)])
    place = (lax.axis_index("feed") * y_count + lax.axis_index("y")).reshape(1)
    core = lax.axis_index("core").reshape(1)
    codes = call(
        tree_kernel,
        "tree",
        (feed_count, y_count, 2, LANES),
        jnp.int32,
        [smem, smem] + [vmem] * 4,
        place,
        core,
        channel_lag.reshape(-1, LANES),
        offsets,
        own,
        other,
    ).reshape(peers, 2, LANES)
    back = lax.all_to_all(codes, ("feed", "y"), split_axis=0, concat_axis=0, tiled=True)
    return call(
        unpack_kernel,
        "unpack",
        (8, 2, channels),
        jnp.float32,
        [vmem],
        back.reshape(peers // 4, 8, LANES),
    )


def solution(mesh):
    devices = mesh.devices
    fine = Mesh(devices.reshape(devices.shape[0], -1, 2), ("feed", "y", "core"))
    high, rest = dft_tables(8 * devices.shape[0])
    times = ("y", "core")
    body = jax.shard_map(
        functools.partial(on_device),
        mesh=fine,
        in_specs=(P(), P(), P(None, "feed", times, None), P(), P()),
        out_specs=P("feed", times, None),
        check_vma=False,
    )

    def run(voltages, channel_lag, offsets):
        return body(jnp.asarray(high), jnp.asarray(rest), voltages, channel_lag, offsets)

    return run
```

```python
import functools
import math

import jax
import jax.numpy as jnp
import ml_dtypes
import numpy as np
from jax import lax
from jax.experimental import pallas as pl
from jax.experimental.pallas import tpu as pltpu
from jax.sharding import Mesh
from jax.sharding import PartitionSpec as P

DS = 2
SECTIONS = 5
GROUP = 2**SECTIONS
LANES = 128
TOP = 14.5
FINE = 800.0
KNEE = -66.0
COARSE = 16.0
KNEE_CODE = (KNEE - TOP) * FINE + 65535.0
LEAST = -126.0
LEAST_CODE = int((LEAST - KNEE) * COARSE + KNEE_CODE)
VMEM_LIMIT = 48 * 1024 * 1024


def dft_tables(feeds):
    hi, big, low = np.meshgrid(np.arange(4), np.arange(feeds // 8), np.arange(2), indexing="ij")
    beam = (8 * big + 2 * hi + low).reshape(-1)
    feed = np.arange(feeds)
    angle = (beam[:, None] * feed[None, :] % feeds) * (2.0 * math.pi / feeds)
    cosine = np.cos(angle) / math.sqrt(feeds)
    sine = np.sin(angle) / math.sqrt(feeds)
    real = np.stack([cosine.reshape(feeds, -1, 8), sine.reshape(feeds, -1, 8)], axis=2)
    imag = np.stack([-sine.reshape(feeds, -1, 8), cosine.reshape(feeds, -1, 8)], axis=2)
    table = np.concatenate([real, imag], axis=0).reshape(2 * feeds, 2 * feeds)
    high = table.astype(ml_dtypes.bfloat16)
    rest = (table - high.astype(np.float64)).astype(ml_dtypes.bfloat16)
    return high, rest


def lane_index(shape):
    return lax.broadcasted_iota(jnp.int32, shape, len(shape) - 1)


def roll(x, by):
    return pltpu.roll(x, by % x.shape[-1], x.ndim - 1)


def swap_blocks(rows):
    lane = lane_index(rows[0].shape)
    low_half = lane < 64
    even = lane % 64 < 32
    turned = [rows[0]] + [roll(rows[n], 32 * n) for n in range(1, 4)]
    out = []
    for g in range(4):
        blocks = [turned[(m - g) % 4] for m in range(4)]
        mixed = jnp.where(
            low_half,
            jnp.where(even, blocks[0], blocks[1]),
            jnp.where(even, blocks[2], blocks[3]),
        )
        out.append(roll(mixed, -32 * g) if g else mixed)
    return out


def encode(x):
    level = jnp.log2(jnp.maximum(x, 2.0**LEAST))
    fine = level * FINE + (65535.5 - TOP * FINE)
    coarse = level * COARSE + (KNEE_CODE + 0.5 - KNEE * COARSE)
    return jnp.maximum(fine, coarse).astype(jnp.int32)


def decode(code):
    value = code.astype(jnp.float32)
    fine = value * (1.0 / FINE) + (TOP - 65535.0 / FINE)
    coarse = value * (1.0 / COARSE) + (KNEE - KNEE_CODE / COARSE)
    return jnp.where(code > LEAST_CODE, jnp.exp2(jnp.minimum(fine, coarse)), 0.0)


def pack_kernel(x_ref, out_ref):
    tiles = x_ref.shape[2] // LANES

    def step(j, _):
        lanes = pl.ds(pl.multiple_of(j * LANES, LANES), LANES)
        rows = [x_ref[n, :, lanes] for n in range(4)]
        for g, value in enumerate(swap_blocks(rows)):
            out_ref[4 * j + g] = value
        return 0

    lax.fori_loop(0, tiles, step, 0, unroll=16)


def beam_kernel(high_ref, rest_ref, x_ref, out_ref):
    sources, blocks, cf, lanes = x_ref.shape
    several = 2
    feeds = high_ref.shape[0] // 2
    rows = feeds // 4
    lane = lane_index((rows, lanes))
    even = lane % 64 < 32
    low_half = lane < 64
    for y in range(0, blocks, several):
        x = jnp.concatenate(
            [x_ref[:, y + k].reshape(sources * cf, lanes) for k in range(several)], axis=1
        )
        beam = jnp.dot(high_ref[...], x, preferred_element_type=jnp.float32)
        beam = beam + jnp.dot(rest_ref[...], x, preferred_element_type=jnp.float32)
        power = beam[:feeds] * beam[:feeds] + beam[feeds:] * beam[feeds:]
        for k in range(several):
            p = [
                power[g * rows : (g + 1) * rows, k * lanes : (k + 1) * lanes] for g in range(4)
            ]
            pairs = []
            for g in (0, 2):
                crossed = jnp.where(even, p[g + 1], p[g])
                crossed = jnp.take_along_axis(crossed, lane ^ 32, axis=1)
                pairs.append(jnp.where(even, p[g], p[g + 1]) + crossed)
            crossed = roll(jnp.where(low_half, pairs[1], pairs[0]), 64)
            first = jnp.where(low_half, pairs[0], crossed)
            second = jnp.where(low_half, crossed, pairs[1])
            out_ref[2 * (y + k)] = (first * (1.0 / DS)).astype(jnp.bfloat16)
            out_ref[2 * (y + k) + 1] = (second * (1.0 / DS)).astype(jnp.bfloat16)


def tree_kernel(place_ref, core_ref, lag_ref, off_ref, own_ref, other_ref, out_ref):
    count = own_ref.shape[0]
    times = 2 * count
    rows = 8
    lane = lane_index((rows, LANES))
    channel = lane % GROUP
    place = place_ref[0]

    per_lag = LANES // GROUP
    lag = jnp.broadcast_to(lag_ref[pl.ds(place // per_lag, 1), :], (rows, LANES))
    lag = jnp.take_along_axis(lag, (place % per_lag) * GROUP + channel, axis=1)
    half_group = GROUP // 2
    per_off = LANES // half_group
    start = pl.multiple_of(place // per_off * LANES, LANES)
    uppers, takes, partners = [], [], []
    for s in range(SECTIONS):
        h = 2**s
        values = jnp.broadcast_to(off_ref[pl.ds(s, 1), pl.ds(start, LANES)], (rows, LANES))
        pair = h * (channel // (2 * h)) + channel % h
        off = jnp.take_along_axis(values, (place % per_off) * half_group + pair, axis=1)
        upper = (channel // h) % 2 == 1
        uppers.append(upper)
        takes.append(jnp.logical_and(upper, off == 1))
        partners.append(jnp.where(upper, lane - h, lane + h))

    zero = jnp.zeros((rows, LANES), jnp.float32)

    def delay(level, late):
        return [
            jnp.where(late, level[t - 1] if t else zero, level[t]) for t in range(times)
        ]

    def run(is_odd):
        def step(k, _):
            at = pl.ds(pl.multiple_of(k * 2 * rows, 2 * rows), 2 * rows)
            for q in range(2):
                level = []
                for t in range(times):
                    mine = (t // 2) % 2 == (1 if is_odd else 0)
                    source = own_ref if mine else other_ref
                    block = source[t // 4 * 2 + t % 2, at, :].astype(jnp.float32)
                    level.append(block[q * rows : (q + 1) * rows])
                level = delay(delay(level, lag >= 1), lag >= 2)
                for s in range(SECTIONS):
                    sent = delay(level, takes[s])
                    after = []
                    for t in range(times):
                        mine = (t // 2) % 2 == (1 if is_odd else 0)
                        if s == SECTIONS - 1 and not mine:
                            after.append(None)
                            continue
                        kept = jnp.where(uppers[s], sent[t - 1] if t else zero, level[t])
                        after.append(kept + jnp.take_along_axis(sent[t], partners[s], axis=1))
                    level = after
                scale = 1.0 / 2**SECTIONS
                for y in range(count // 2):
                    t = 4 * y + (2 if is_odd else 0)
                    word = encode(level[t] * scale) | (encode(level[t + 1] * scale) << 16)
                    for i in range(rows // 2):
                        out_ref[(2 * k + q) * (rows // 2) + i, y] = word[2 * i : 2 * i + 2]
            return 0

        lax.fori_loop(0, own_ref.shape[1] // (2 * rows), step, 0)

    @pl.when(core_ref[0] == 0)
    def _():
        run(False)

    @pl.when(core_ref[0] != 0)
    def _():
        run(True)


def unpack_kernel(x_ref, out_ref):
    tiles = x_ref.shape[0]
    lane = lane_index((8, LANES))
    row = lax.broadcasted_iota(jnp.int32, (8, LANES), 0)
    stay_far = (row < 4) == (lane < 64)
    stay_near = (row % 4 < 2) == (lane % 64 < 32)

    def step(j, _):
        v = x_ref[j]
        u = jnp.where(stay_far, v, roll(pltpu.roll(v, 4, 0), 64))
        moved = jnp.take_along_axis(u, row ^ 2, axis=0)
        moved = jnp.take_along_axis(moved, lane ^ 32, axis=1)
        w = jnp.where(stay_near, u, moved)
        lanes = pl.ds(pl.multiple_of(j * LANES, LANES), LANES)
        for k in range(2):
            twice = jnp.take_along_axis(w, row // 2 + 4 * k, axis=0)
            value = decode(jnp.where(row % 2 == 1, twice >> 16, twice) & 65535)
            out_ref[4 * k : 4 * k + 4, :, lanes] = value.reshape(4, 2, LANES)
        return 0

    lax.fori_loop(0, tiles, step, 0, unroll=32)


def on_device(high, rest, voltages, channel_lag, offsets):
    parts, local, samp, channels = voltages.shape
    feed_count = lax.axis_size("feed")
    y_count = lax.axis_size("y")
    peers = feed_count * y_count
    cf = parts * local
    params = pltpu.CompilerParams(vmem_limit_bytes=VMEM_LIMIT)
    vmem = pl.BlockSpec(memory_space=pltpu.VMEM)
    smem = pl.BlockSpec(memory_space=pltpu.SMEM)

    def call(kernel, name, shape, dtype, specs, *operands):
        return pl.pallas_call(
            kernel,
            in_specs=specs,
            out_specs=vmem,
            out_shape=jax.ShapeDtypeStruct(shape, dtype),
            compiler_params=params,
            name=name,
        )(*operands)

    rows = voltages.reshape(cf, samp, channels).transpose(1, 0, 2)
    packed = call(pack_kernel, "pack", (peers, cf, LANES), jnp.bfloat16, [vmem], rows)
    turned = lax.all_to_all(packed, ("feed", "y"), split_axis=0, concat_axis=0, tiled=True)
    turned = turned.reshape(feed_count, y_count, cf, LANES)
    beams = feed_count * local
    own = call(
        beam_kernel,
        "beams",
        (2 * y_count, beams // 4, LANES),
        jnp.bfloat16,
        [vmem] * 3,
        high,
        rest,
        turned,
    )
    other = lax.ppermute(own, "core", [(0, 1), (1, 0)])
    place = (lax.axis_index("feed") * y_count + lax.axis_index("y")).reshape(1)
    core = lax.axis_index("core").reshape(1)
    codes = call(
        tree_kernel,
        "tree",
        (feed_count, y_count, 2, LANES),
        jnp.int32,
        [smem, smem] + [vmem] * 4,
        place,
        core,
        channel_lag.reshape(-1, LANES),
        offsets,
        own,
        other,
    ).reshape(peers, 2, LANES)
    back = lax.all_to_all(codes, ("feed", "y"), split_axis=0, concat_axis=0, tiled=True)
    return call(
        unpack_kernel,
        "unpack",
        (8, 2, channels),
        jnp.float32,
        [vmem],
        back.reshape(peers // 4, 8, LANES),
    )


def solution(mesh):
    devices = mesh.devices
    fine = Mesh(devices.reshape(devices.shape[0], -1, 2), ("feed", "y", "core"))
    high, rest = dft_tables(8 * devices.shape[0])
    times = ("y", "core")
    body = jax.shard_map(
        functools.partial(on_device),
        mesh=fine,
        in_specs=(P(), P(), P(None, "feed", times, None), P(), P()),
        out_specs=P("feed", times, None),
        check_vma=False,
    )

    def run(voltages, channel_lag, offsets):
        return body(jnp.asarray(high), jnp.asarray(rest), voltages, channel_lag, offsets)

    return run
```

```python
import functools
import math

import jax
import jax.numpy as jnp
import ml_dtypes
import numpy as np
from jax import lax
from jax.experimental import pallas as pl
from jax.experimental.pallas import tpu as pltpu
from jax.sharding import Mesh
from jax.sharding import PartitionSpec as P

DS = 2
SECTIONS = 5
GROUP = 2**SECTIONS
LANES = 128
TOP = 14.5
FINE = 800.0
KNEE = -66.0
COARSE = 16.0
KNEE_CODE = (KNEE - TOP) * FINE + 65535.0
LEAST = -126.0
LEAST_CODE = int((LEAST - KNEE) * COARSE + KNEE_CODE)
VMEM_LIMIT = 48 * 1024 * 1024


def dft_tables(feeds):
    hi, big, low = np.meshgrid(np.arange(4), np.arange(feeds // 8), np.arange(2), indexing="ij")
    beam = (8 * big + 2 * hi + low).reshape(-1)
    feed = np.arange(feeds)
    angle = (beam[:, None] * feed[None, :] % feeds) * (2.0 * math.pi / feeds)
    cosine = np.cos(angle) / math.sqrt(feeds)
    sine = np.sin(angle) / math.sqrt(feeds)
    real = np.stack([cosine.reshape(feeds, -1, 8), sine.reshape(feeds, -1, 8)], axis=2)
    imag = np.stack([-sine.reshape(feeds, -1, 8), cosine.reshape(feeds, -1, 8)], axis=2)
    table = np.concatenate([real, imag], axis=0).reshape(2 * feeds, 2 * feeds)
    high = table.astype(ml_dtypes.bfloat16)
    rest = (table - high.astype(np.float64)).astype(ml_dtypes.bfloat16)
    return high, rest


def lane_index(shape):
    return lax.broadcasted_iota(jnp.int32, shape, len(shape) - 1)


def roll(x, by):
    return pltpu.roll(x, by % x.shape[-1], x.ndim - 1)


def swap_blocks(rows):
    lane = lane_index(rows[0].shape)
    low_half = lane < 64
    even = lane % 64 < 32
    turned = [rows[0]] + [roll(rows[n], 32 * n) for n in range(1, 4)]
    out = []
    for g in range(4):
        blocks = [turned[(m - g) % 4] for m in range(4)]
        mixed = jnp.where(
            low_half,
            jnp.where(even, blocks[0], blocks[1]),
            jnp.where(even, blocks[2], blocks[3]),
        )
        out.append(roll(mixed, -32 * g) if g else mixed)
    return out


def encode(x):
    level = jnp.log2(jnp.maximum(x, 2.0**LEAST))
    fine = level * FINE + (65535.5 - TOP * FINE)
    coarse = level * COARSE + (KNEE_CODE + 0.5 - KNEE * COARSE)
    return jnp.maximum(fine, coarse).astype(jnp.int32)


def decode(code):
    value = code.astype(jnp.float32)
    fine = value * (1.0 / FINE) + (TOP - 65535.0 / FINE)
    coarse = value * (1.0 / COARSE) + (KNEE - KNEE_CODE / COARSE)
    return jnp.where(code > LEAST_CODE, jnp.exp2(jnp.minimum(fine, coarse)), 0.0)


def pack_kernel(x_ref, out_ref):
    tiles = x_ref.shape[2] // LANES

    def step(j, _):
        lanes = pl.ds(pl.multiple_of(j * LANES, LANES), LANES)
        rows = [x_ref[n, :, lanes] for n in range(4)]
        for g, value in enumerate(swap_blocks(rows)):
            out_ref[4 * j + g] = value
        return 0

    lax.fori_loop(0, tiles, step, 0, unroll=16)


def beam_kernel(high_ref, rest_ref, x_ref, out_ref):
    blocks, sources, cf, lanes = x_ref.shape
    several = 2
    feeds = high_ref.shape[0] // 2
    rows = feeds // 4
    lane = lane_index((rows, lanes))
    even = lane % 64 < 32
    low_half = lane < 64
    for y in range(0, blocks, several):
        x = jnp.concatenate(
            [x_ref[y + k].reshape(sources * cf, lanes) for k in range(several)], axis=1
        )
        beam = jnp.dot(high_ref[...], x, preferred_element_type=jnp.float32)
        beam = beam + jnp.dot(rest_ref[...], x, preferred_element_type=jnp.float32)
        power = beam[:feeds] * beam[:feeds] + beam[feeds:] * beam[feeds:]
        for k in range(several):
            p = [
                power[g * rows : (g + 1) * rows, k * lanes : (k + 1) * lanes] for g in range(4)
            ]
            pairs = []
            for g in (0, 2):
                crossed = jnp.where(even, p[g + 1], p[g])
                crossed = jnp.take_along_axis(crossed, lane ^ 32, axis=1)
                pairs.append(jnp.where(even, p[g], p[g + 1]) + crossed)
            crossed = roll(jnp.where(low_half, pairs[1], pairs[0]), 64)
            first = jnp.where(low_half, pairs[0], crossed)
            second = jnp.where(low_half, crossed, pairs[1])
            out_ref[2 * (y + k)] = (first * (1.0 / DS)).astype(jnp.bfloat16)
            out_ref[2 * (y + k) + 1] = (second * (1.0 / DS)).astype(jnp.bfloat16)


def tree_kernel(place_ref, core_ref, lag_ref, off_ref, own_ref, other_ref, out_ref):
    count = own_ref.shape[0]
    times = 2 * count
    rows = 8
    lane = lane_index((rows, LANES))
    channel = lane % GROUP
    place = place_ref[0]

    per_lag = LANES // GROUP
    lag = jnp.broadcast_to(lag_ref[pl.ds(place // per_lag, 1), :], (rows, LANES))
    lag = jnp.take_along_axis(lag, (place % per_lag) * GROUP + channel, axis=1)
    half_group = GROUP // 2
    per_off = LANES // half_group
    start = pl.multiple_of(place // per_off * LANES, LANES)
    uppers, takes, partners = [], [], []
    for s in range(SECTIONS):
        h = 2**s
        values = jnp.broadcast_to(off_ref[pl.ds(s, 1), pl.ds(start, LANES)], (rows, LANES))
        pair = h * (channel // (2 * h)) + channel % h
        off = jnp.take_along_axis(values, (place % per_off) * half_group + pair, axis=1)
        upper = (channel // h) % 2 == 1
        uppers.append(upper)
        takes.append(jnp.logical_and(upper, off == 1))
        partners.append(jnp.where(upper, lane - h, lane + h))

    zero = jnp.zeros((rows, LANES), jnp.float32)

    def delay(level, late):
        return [
            jnp.where(late, level[t - 1] if t else zero, level[t]) for t in range(times)
        ]

    def run(is_odd):
        def step(k, _):
            at = pl.ds(pl.multiple_of(k * 2 * rows, 2 * rows), 2 * rows)
            for q in range(2):
                level = []
                for t in range(times):
                    mine = (t // 2) % 2 == (1 if is_odd else 0)
                    source = own_ref if mine else other_ref
                    block = source[t // 4 * 2 + t % 2, at, :].astype(jnp.float32)
                    level.append(block[q * rows : (q + 1) * rows])
                level = delay(delay(level, lag >= 1), lag >= 2)
                for s in range(SECTIONS):
                    sent = delay(level, takes[s])
                    after = []
                    for t in range(times):
                        mine = (t // 2) % 2 == (1 if is_odd else 0)
                        if s == SECTIONS - 1 and not mine:
                            after.append(None)
                            continue
                        kept = jnp.where(uppers[s], sent[t - 1] if t else zero, level[t])
                        after.append(kept + jnp.take_along_axis(sent[t], partners[s], axis=1))
                    level = after
                scale = 1.0 / 2**SECTIONS
                for y in range(count // 2):
                    t = 4 * y + (2 if is_odd else 0)
                    word = encode(level[t] * scale) | (encode(level[t + 1] * scale) << 16)
                    out_ref[y, 2 * k + q] = word
            return 0

        lax.fori_loop(0, own_ref.shape[1] // (2 * rows), step, 0)

    @pl.when(core_ref[0] == 0)
    def _():
        run(False)

    @pl.when(core_ref[0] != 0)
    def _():
        run(True)


def unpack_kernel(x_ref, out_ref):
    tiles = x_ref.shape[0]
    lane = lane_index((8, LANES))
    row = lax.broadcasted_iota(jnp.int32, (8, LANES), 0)
    stay_far = (row < 4) == (lane < 64)
    stay_near = (row % 4 < 2) == (lane % 64 < 32)

    def step(j, _):
        v = x_ref[j]
        u = jnp.where(stay_far, v, roll(pltpu.roll(v, 4, 0), 64))
        moved = jnp.take_along_axis(u, row ^ 2, axis=0)
        moved = jnp.take_along_axis(moved, lane ^ 32, axis=1)
        w = jnp.where(stay_near, u, moved)
        lanes = pl.ds(pl.multiple_of(j * LANES, LANES), LANES)
        for k in range(2):
            twice = jnp.take_along_axis(w, row // 2 + 4 * k, axis=0)
            value = decode(jnp.where(row % 2 == 1, twice >> 16, twice) & 65535)
            out_ref[4 * k : 4 * k + 4, :, lanes] = value.reshape(4, 2, LANES)
        return 0

    lax.fori_loop(0, tiles, step, 0, unroll=32)


def on_device(high, rest, voltages, channel_lag, offsets):
    parts, local, samp, channels = voltages.shape
    feed_count = lax.axis_size("feed")
    y_count = lax.axis_size("y")
    peers = feed_count * y_count
    cf = parts * local
    params = pltpu.CompilerParams(vmem_limit_bytes=VMEM_LIMIT)
    vmem = pl.BlockSpec(memory_space=pltpu.VMEM)
    smem = pl.BlockSpec(memory_space=pltpu.SMEM)

    def call(kernel, name, shape, dtype, specs, *operands):
        return pl.pallas_call(
            kernel,
            in_specs=specs,
            out_specs=vmem,
            out_shape=jax.ShapeDtypeStruct(shape, dtype),
            compiler_params=params,
            name=name,
        )(*operands)

    rows = voltages.reshape(cf, samp, channels).transpose(1, 0, 2)
    packed = call(pack_kernel, "pack", (peers, cf, LANES), jnp.bfloat16, [vmem], rows)
    turned = lax.all_to_all(packed, ("y", "feed"), split_axis=0, concat_axis=0, tiled=True)
    turned = turned.reshape(y_count, feed_count, cf, LANES)
    beams = feed_count * local
    own = call(
        beam_kernel,
        "beams",
        (2 * y_count, beams // 4, LANES),
        jnp.bfloat16,
        [vmem] * 3,
        high,
        rest,
        turned,
    )
    other = lax.ppermute(own, "core", [(0, 1), (1, 0)])
    place = (lax.axis_index("y") * feed_count + lax.axis_index("feed")).reshape(1)
    core = lax.axis_index("core").reshape(1)
    codes = call(
        tree_kernel,
        "tree",
        (y_count, feed_count // 4, 8, LANES),
        jnp.int32,
        [smem, smem] + [vmem] * 4,
        place,
        core,
        channel_lag.reshape(-1, LANES),
        offsets,
        own,
        other,
    ).reshape(peers, 2, LANES)
    back = lax.all_to_all(codes, ("y", "feed"), split_axis=0, concat_axis=0, tiled=True)
    return call(
        unpack_kernel,
        "unpack",
        (8, 2, channels),
        jnp.float32,
        [vmem],
        back.reshape(peers // 4, 8, LANES),
    )


def solution(mesh):
    devices = mesh.devices
    fine = Mesh(devices.reshape(devices.shape[0], -1, 2), ("feed", "y", "core"))
    high, rest = dft_tables(8 * devices.shape[0])
    times = ("y", "core")
    body = jax.shard_map(
        functools.partial(on_device),
        mesh=fine,
        in_specs=(P(), P(), P(None, "feed", times, None), P(), P()),
        out_specs=P("feed", times, None),
        check_vma=False,
    )

    def run(voltages, channel_lag, offsets):
        return body(jnp.asarray(high), jnp.asarray(rest), voltages, channel_lag, offsets)

    return run
```

```python
import functools
import math

import jax
import jax.numpy as jnp
import ml_dtypes
import numpy as np
from jax import lax
from jax.experimental import pallas as pl
from jax.experimental.pallas import tpu as pltpu
from jax.sharding import Mesh
from jax.sharding import PartitionSpec as P

FEED = ("z2", "z1", "z0", "x")
TIME = ("y2", "y1", "y0", "core")
PEERS = ("z2", "y2", "z1", "y1", "z0", "y0", "x")
DS = 2
SECTIONS = 5
GROUP = 2**SECTIONS
LANES = 128
TOP = 14.5
FINE = 800.0
KNEE = -66.0
COARSE = 16.0
KNEE_CODE = (KNEE - TOP) * FINE + 65535.0
LEAST = -126.0
LEAST_CODE = int((LEAST - KNEE) * COARSE + KNEE_CODE)
VMEM_LIMIT = 48 * 1024 * 1024


def dft_tables(feeds):
    hi, big, low = np.meshgrid(np.arange(4), np.arange(feeds // 8), np.arange(2), indexing="ij")
    beam = (8 * big + 2 * hi + low).reshape(-1)
    feed = np.arange(feeds)
    angle = (beam[:, None] * feed[None, :] % feeds) * (2.0 * math.pi / feeds)
    cosine = np.cos(angle) / math.sqrt(feeds)
    sine = np.sin(angle) / math.sqrt(feeds)
    real = np.stack([cosine.reshape(feeds, -1, 8), sine.reshape(feeds, -1, 8)], axis=2)
    imag = np.stack([-sine.reshape(feeds, -1, 8), cosine.reshape(feeds, -1, 8)], axis=2)
    table = np.concatenate([real, imag], axis=0).reshape(2 * feeds, 2 * feeds)
    high = table.astype(ml_dtypes.bfloat16)
    rest = (table - high.astype(np.float64)).astype(ml_dtypes.bfloat16)
    return high, rest


def woven(z, y):
    total = 0
    for bit in range(3):
        total = total + (z >> bit) % 2 * 2 ** (2 * bit + 1) + (y >> bit) % 2 * 2 ** (2 * bit)
    return total


def lane_index(shape):
    return lax.broadcasted_iota(jnp.int32, shape, len(shape) - 1)


def roll(x, by):
    return pltpu.roll(x, by % x.shape[-1], x.ndim - 1)


def swap_blocks(rows):
    lane = lane_index(rows[0].shape)
    low_half = lane < 64
    even = lane % 64 < 32
    turned = [rows[0]] + [roll(rows[n], 32 * n) for n in range(1, 4)]
    out = []
    for g in range(4):
        blocks = [turned[(m - g) % 4] for m in range(4)]
        mixed = jnp.where(
            low_half,
            jnp.where(even, blocks[0], blocks[1]),
            jnp.where(even, blocks[2], blocks[3]),
        )
        out.append(roll(mixed, -32 * g) if g else mixed)
    return out


def encode(x):
    level = jnp.log2(jnp.maximum(x, 2.0**LEAST))
    fine = level * FINE + (65535.5 - TOP * FINE)
    coarse = level * COARSE + (KNEE_CODE + 0.5 - KNEE * COARSE)
    return jnp.maximum(fine, coarse).astype(jnp.int32)


def decode(code):
    value = code.astype(jnp.float32)
    fine = value * (1.0 / FINE) + (TOP - 65535.0 / FINE)
    coarse = value * (1.0 / COARSE) + (KNEE - KNEE_CODE / COARSE)
    return jnp.where(code > LEAST_CODE, jnp.exp2(jnp.minimum(fine, coarse)), 0.0)


def pack_kernel(x_ref, out_ref):
    tiles = x_ref.shape[2] // LANES

    def step(j, _):
        lanes = pl.ds(pl.multiple_of(j * LANES, LANES), LANES)
        rows = [x_ref[n, :, lanes] for n in range(4)]
        for g, value in enumerate(swap_blocks(rows)):
            out_ref[4 * j + g] = value
        return 0

    lax.fori_loop(0, tiles, step, 0, unroll=16)


def beam_kernel(high_ref, rest_ref, x_ref, out_ref):
    blocks = 8
    _, few, cf, lanes = x_ref.shape
    several = 2
    feeds = high_ref.shape[0] // 2
    rows = feeds // 4
    lane = lane_index((rows, lanes))
    even = lane % 64 < 32
    low_half = lane < 64
    for y in range(0, blocks, several):
        x = jnp.concatenate(
            [
                jnp.concatenate(
                    [x_ref[woven(z, y + k)].reshape(few * cf, lanes) for z in range(8)], axis=0
                )
                for k in range(several)
            ],
            axis=1,
        )
        beam = jnp.dot(high_ref[...], x, preferred_element_type=jnp.float32)
        beam = beam + jnp.dot(rest_ref[...], x, preferred_element_type=jnp.float32)
        power = beam[:feeds] * beam[:feeds] + beam[feeds:] * beam[feeds:]
        for k in range(several):
            p = [
                power[g * rows : (g + 1) * rows, k * lanes : (k + 1) * lanes] for g in range(4)
            ]
            pairs = []
            for g in (0, 2):
                crossed = jnp.where(even, p[g + 1], p[g])
                crossed = jnp.take_along_axis(crossed, lane ^ 32, axis=1)
                pairs.append(jnp.where(even, p[g], p[g + 1]) + crossed)
            crossed = roll(jnp.where(low_half, pairs[1], pairs[0]), 64)
            first = jnp.where(low_half, pairs[0], crossed)
            second = jnp.where(low_half, crossed, pairs[1])
            out_ref[2 * (y + k)] = (first * (1.0 / DS)).astype(jnp.bfloat16)
            out_ref[2 * (y + k) + 1] = (second * (1.0 / DS)).astype(jnp.bfloat16)


def tree_kernel(place_ref, core_ref, lag_ref, off_ref, own_ref, other_ref, out_ref):
    count = own_ref.shape[0]
    times = 2 * count
    rows = 8
    lane = lane_index((rows, LANES))
    channel = lane % GROUP
    place = place_ref[0]

    per_lag = LANES // GROUP
    lag = jnp.broadcast_to(lag_ref[pl.ds(place // per_lag, 1), :], (rows, LANES))
    lag = jnp.take_along_axis(lag, (place % per_lag) * GROUP + channel, axis=1)
    half_group = GROUP // 2
    per_off = LANES // half_group
    start = pl.multiple_of(place // per_off * LANES, LANES)
    uppers, takes, partners = [], [], []
    for s in range(SECTIONS):
        h = 2**s
        values = jnp.broadcast_to(off_ref[pl.ds(s, 1), pl.ds(start, LANES)], (rows, LANES))
        pair = h * (channel // (2 * h)) + channel % h
        off = jnp.take_along_axis(values, (place % per_off) * half_group + pair, axis=1)
        upper = (channel // h) % 2 == 1
        uppers.append(upper)
        takes.append(jnp.logical_and(upper, off == 1))
        partners.append(jnp.where(upper, lane - h, lane + h))

    zero = jnp.zeros((rows, LANES), jnp.float32)

    def delay(level, late):
        return [
            jnp.where(late, level[t - 1] if t else zero, level[t]) for t in range(times)
        ]

    def run(is_odd):
        def step(k, _):
            at = pl.ds(pl.multiple_of(k * 2 * rows, 2 * rows), 2 * rows)
            for q in range(2):
                level = []
                for t in range(times):
                    mine = (t // 2) % 2 == (1 if is_odd else 0)
                    source = own_ref if mine else other_ref
                    block = source[t // 4 * 2 + t % 2, at, :].astype(jnp.float32)
                    level.append(block[q * rows : (q + 1) * rows])
                level = delay(delay(level, lag >= 1), lag >= 2)
                for s in range(SECTIONS):
                    sent = delay(level, takes[s])
                    after = []
                    for t in range(times):
                        mine = (t // 2) % 2 == (1 if is_odd else 0)
                        if s == SECTIONS - 1 and not mine:
                            after.append(None)
                            continue
                        kept = jnp.where(uppers[s], sent[t - 1] if t else zero, level[t])
                        after.append(kept + jnp.take_along_axis(sent[t], partners[s], axis=1))
                    level = after
                scale = 1.0 / 2**SECTIONS
                for y in range(count // 2):
                    t = 4 * y + (2 if is_odd else 0)
                    word = encode(level[t] * scale) | (encode(level[t + 1] * scale) << 16)
                    out_ref[woven(2 * k + q, y)] = word
            return 0

        lax.fori_loop(0, own_ref.shape[1] // (2 * rows), step, 0)

    @pl.when(core_ref[0] == 0)
    def _():
        run(False)

    @pl.when(core_ref[0] != 0)
    def _():
        run(True)


def unpack_kernel(x_ref, out_ref):
    tiles = x_ref.shape[0]
    lane = lane_index((8, LANES))
    row = lax.broadcasted_iota(jnp.int32, (8, LANES), 0)
    stay_far = (row < 4) == (lane < 64)
    stay_near = (row % 4 < 2) == (lane % 64 < 32)

    def step(j, _):
        v = x_ref[j]
        u = jnp.where(stay_far, v, roll(pltpu.roll(v, 4, 0), 64))
        moved = jnp.take_along_axis(u, row ^ 2, axis=0)
        moved = jnp.take_along_axis(moved, lane ^ 32, axis=1)
        w = jnp.where(stay_near, u, moved)
        lanes = pl.ds(pl.multiple_of(j * LANES, LANES), LANES)
        for k in range(2):
            twice = jnp.take_along_axis(w, row // 2 + 4 * k, axis=0)
            value = decode(jnp.where(row % 2 == 1, twice >> 16, twice) & 65535)
            out_ref[4 * k : 4 * k + 4, :, lanes] = value.reshape(4, 2, LANES)
        return 0

    lax.fori_loop(0, tiles, step, 0, unroll=32)


def on_device(high, rest, voltages, channel_lag, offsets):
    parts, local, samp, channels = voltages.shape
    feed_count, y_count = 32, 8
    peers = feed_count * y_count
    cf = parts * local
    params = pltpu.CompilerParams(vmem_limit_bytes=VMEM_LIMIT)
    vmem = pl.BlockSpec(memory_space=pltpu.VMEM)
    smem = pl.BlockSpec(memory_space=pltpu.SMEM)

    def call(kernel, name, shape, dtype, specs, *operands):
        return pl.pallas_call(
            kernel,
            in_specs=specs,
            out_specs=vmem,
            out_shape=jax.ShapeDtypeStruct(shape, dtype),
            compiler_params=params,
            name=name,
        )(*operands)

    rows = voltages.reshape(cf, samp, channels).transpose(1, 0, 2)
    packed = call(pack_kernel, "pack", (peers, cf, LANES), jnp.bfloat16, [vmem], rows)
    turned = lax.all_to_all(packed, PEERS, split_axis=0, concat_axis=0, tiled=True)
    turned = turned.reshape(peers // 4, 4, cf, LANES)
    beams = feed_count * local
    own = call(
        beam_kernel,
        "beams",
        (2 * y_count, beams // 4, LANES),
        jnp.bfloat16,
        [vmem] * 3,
        high,
        rest,
        turned,
    )
    other = lax.ppermute(own, "core", [(0, 1), (1, 0)])
    place = lax.axis_index(PEERS).reshape(1)
    core = lax.axis_index("core").reshape(1)
    codes = call(
        tree_kernel,
        "tree",
        (peers // 4, 8, LANES),
        jnp.int32,
        [smem, smem] + [vmem] * 4,
        place,
        core,
        channel_lag.reshape(-1, LANES),
        offsets,
        own,
        other,
    ).reshape(peers, 2, LANES)
    back = lax.all_to_all(codes, PEERS, split_axis=0, concat_axis=0, tiled=True)
    return call(
        unpack_kernel,
        "unpack",
        (8, 2, channels),
        jnp.float32,
        [vmem],
        back.reshape(peers // 4, 8, LANES),
    )


def solution(mesh):
    devices = mesh.devices
    fine = Mesh(devices.reshape((2, 2, 2, 4, 2, 2, 2, 2)), FEED + TIME)
    high, rest = dft_tables(8 * devices.shape[0])
    body = jax.shard_map(
        functools.partial(on_device),
        mesh=fine,
        in_specs=(P(), P(), P(None, FEED, TIME, None), P(), P()),
        out_specs=P(FEED, TIME, None),
        check_vma=False,
    )

    def run(voltages, channel_lag, offsets):
        return body(jnp.asarray(high), jnp.asarray(rest), voltages, channel_lag, offsets)

    return run
```

```python
import functools
import math

import jax
import jax.numpy as jnp
import ml_dtypes
import numpy as np
from jax import lax
from jax.experimental import pallas as pl
from jax.experimental.pallas import tpu as pltpu
from jax.sharding import Mesh
from jax.sharding import PartitionSpec as P

FEED = ("z", "x")
TIME = ("y", "core")
PEERS = ("x", "z", "y")
DS = 2
SECTIONS = 5
GROUP = 2**SECTIONS
LANES = 128
TOP = 14.5
FINE = 800.0
KNEE = -66.0
COARSE = 16.0
KNEE_CODE = (KNEE - TOP) * FINE + 65535.0
LEAST = -126.0
LEAST_CODE = int((LEAST - KNEE) * COARSE + KNEE_CODE)
VMEM_LIMIT = 48 * 1024 * 1024


def dft_tables(feeds):
    hi, big, low = np.meshgrid(np.arange(4), np.arange(feeds // 8), np.arange(2), indexing="ij")
    beam = (8 * big + 2 * hi + low).reshape(-1)
    feed = np.arange(feeds)
    angle = (beam[:, None] * feed[None, :] % feeds) * (2.0 * math.pi / feeds)
    cosine = np.cos(angle) / math.sqrt(feeds)
    sine = np.sin(angle) / math.sqrt(feeds)
    real = np.stack([cosine.reshape(feeds, -1, 8), sine.reshape(feeds, -1, 8)], axis=2)
    imag = np.stack([-sine.reshape(feeds, -1, 8), cosine.reshape(feeds, -1, 8)], axis=2)
    table = np.concatenate([real, imag], axis=0).reshape(2 * feeds, 2 * feeds)
    high = table.astype(ml_dtypes.bfloat16)
    rest = (table - high.astype(np.float64)).astype(ml_dtypes.bfloat16)
    return high, rest


def lane_index(shape):
    return lax.broadcasted_iota(jnp.int32, shape, len(shape) - 1)


def roll(x, by):
    return pltpu.roll(x, by % x.shape[-1], x.ndim - 1)


def swap_blocks(rows):
    lane = lane_index(rows[0].shape)
    low_half = lane < 64
    even = lane % 64 < 32
    turned = [rows[0]] + [roll(rows[n], 32 * n) for n in range(1, 4)]
    out = []
    for g in range(4):
        blocks = [turned[(m - g) % 4] for m in range(4)]
        mixed = jnp.where(
            low_half,
            jnp.where(even, blocks[0], blocks[1]),
            jnp.where(even, blocks[2], blocks[3]),
        )
        out.append(roll(mixed, -32 * g) if g else mixed)
    return out


def encode(x):
    level = jnp.log2(jnp.maximum(x, 2.0**LEAST))
    fine = level * FINE + (65535.5 - TOP * FINE)
    coarse = level * COARSE + (KNEE_CODE + 0.5 - KNEE * COARSE)
    return jnp.maximum(fine, coarse).astype(jnp.int32)


def decode(code):
    value = code.astype(jnp.float32)
    fine = value * (1.0 / FINE) + (TOP - 65535.0 / FINE)
    coarse = value * (1.0 / COARSE) + (KNEE - KNEE_CODE / COARSE)
    return jnp.where(code > LEAST_CODE, jnp.exp2(jnp.minimum(fine, coarse)), 0.0)


def pack_kernel(x_ref, out_ref):
    tiles = x_ref.shape[2] // LANES

    def step(j, _):
        lanes = pl.ds(pl.multiple_of(j * LANES, LANES), LANES)
        rows = [x_ref[n, :, lanes] for n in range(4)]
        for g, value in enumerate(swap_blocks(rows)):
            out_ref[4 * j + g] = value
        return 0

    lax.fori_loop(0, tiles, step, 0, unroll=16)


def beam_kernel(high_ref, rest_ref, x_ref, out_ref):
    blocks, lanes = 8, LANES
    several = 2
    feeds = high_ref.shape[0] // 2
    rows = feeds // 4
    lane = lane_index((rows, lanes))
    even = lane % 64 < 32
    low_half = lane < 64
    for y in range(0, blocks, several):
        x = jnp.concatenate(
            [
                jnp.concatenate(
                    [x_ref[x, z, y + k] for z in range(8) for x in range(4)], axis=0
                )
                for k in range(several)
            ],
            axis=1,
        )
        beam = jnp.dot(high_ref[...], x, preferred_element_type=jnp.float32)
        beam = beam + jnp.dot(rest_ref[...], x, preferred_element_type=jnp.float32)
        power = beam[:feeds] * beam[:feeds] + beam[feeds:] * beam[feeds:]
        for k in range(several):
            p = [
                power[g * rows : (g + 1) * rows, k * lanes : (k + 1) * lanes] for g in range(4)
            ]
            pairs = []
            for g in (0, 2):
                crossed = jnp.where(even, p[g + 1], p[g])
                crossed = jnp.take_along_axis(crossed, lane ^ 32, axis=1)
                pairs.append(jnp.where(even, p[g], p[g + 1]) + crossed)
            crossed = roll(jnp.where(low_half, pairs[1], pairs[0]), 64)
            first = jnp.where(low_half, pairs[0], crossed)
            second = jnp.where(low_half, crossed, pairs[1])
            out_ref[2 * (y + k)] = (first * (1.0 / DS)).astype(jnp.bfloat16)
            out_ref[2 * (y + k) + 1] = (second * (1.0 / DS)).astype(jnp.bfloat16)


def tree_kernel(place_ref, core_ref, lag_ref, off_ref, own_ref, other_ref, out_ref):
    count = own_ref.shape[0]
    times = 2 * count
    rows = 8
    lane = lane_index((rows, LANES))
    channel = lane % GROUP
    place = place_ref[0]

    per_lag = LANES // GROUP
    lag = jnp.broadcast_to(lag_ref[pl.ds(place // per_lag, 1), :], (rows, LANES))
    lag = jnp.take_along_axis(lag, (place % per_lag) * GROUP + channel, axis=1)
    half_group = GROUP // 2
    per_off = LANES // half_group
    start = pl.multiple_of(place // per_off * LANES, LANES)
    uppers, takes, partners = [], [], []
    for s in range(SECTIONS):
        h = 2**s
        values = jnp.broadcast_to(off_ref[pl.ds(s, 1), pl.ds(start, LANES)], (rows, LANES))
        pair = h * (channel // (2 * h)) + channel % h
        off = jnp.take_along_axis(values, (place % per_off) * half_group + pair, axis=1)
        upper = (channel // h) % 2 == 1
        uppers.append(upper)
        takes.append(jnp.logical_and(upper, off == 1))
        partners.append(jnp.where(upper, lane - h, lane + h))

    zero = jnp.zeros((rows, LANES), jnp.float32)

    def delay(level, late):
        return [
            jnp.where(late, level[t - 1] if t else zero, level[t]) for t in range(times)
        ]

    def run(is_odd):
        def step(k, _):
            at = pl.ds(pl.multiple_of(k * 2 * rows, 2 * rows), 2 * rows)
            for q in range(2):
                level = []
                for t in range(times):
                    mine = (t // 2) % 2 == (1 if is_odd else 0)
                    source = own_ref if mine else other_ref
                    block = source[t // 4 * 2 + t % 2, at, :].astype(jnp.float32)
                    level.append(block[q * rows : (q + 1) * rows])
                level = delay(delay(level, lag >= 1), lag >= 2)
                for s in range(SECTIONS):
                    sent = delay(level, takes[s])
                    after = []
                    for t in range(times):
                        mine = (t // 2) % 2 == (1 if is_odd else 0)
                        if s == SECTIONS - 1 and not mine:
                            after.append(None)
                            continue
                        kept = jnp.where(uppers[s], sent[t - 1] if t else zero, level[t])
                        after.append(kept + jnp.take_along_axis(sent[t], partners[s], axis=1))
                    level = after
                scale = 1.0 / 2**SECTIONS
                for y in range(count // 2):
                    t = 4 * y + (2 if is_odd else 0)
                    word = encode(level[t] * scale) | (encode(level[t + 1] * scale) << 16)
                    for x in range(4):
                        out_ref[x, 2 * k + q, y] = word[2 * x : 2 * x + 2]
            return 0

        lax.fori_loop(0, own_ref.shape[1] // (2 * rows), step, 0)

    @pl.when(core_ref[0] == 0)
    def _():
        run(False)

    @pl.when(core_ref[0] != 0)
    def _():
        run(True)


def unpack_kernel(x_ref, out_ref):
    tiles = x_ref.shape[0]
    lane = lane_index((8, LANES))
    row = lax.broadcasted_iota(jnp.int32, (8, LANES), 0)
    stay_far = (row < 4) == (lane < 64)
    stay_near = (row % 4 < 2) == (lane % 64 < 32)

    def step(j, _):
        v = x_ref[j]
        u = jnp.where(stay_far, v, roll(pltpu.roll(v, 4, 0), 64))
        moved = jnp.take_along_axis(u, row ^ 2, axis=0)
        moved = jnp.take_along_axis(moved, lane ^ 32, axis=1)
        w = jnp.where(stay_near, u, moved)
        lanes = pl.ds(pl.multiple_of(j * LANES, LANES), LANES)
        for k in range(2):
            twice = jnp.take_along_axis(w, row // 2 + 4 * k, axis=0)
            value = decode(jnp.where(row % 2 == 1, twice >> 16, twice) & 65535)
            out_ref[4 * k : 4 * k + 4, :, lanes] = value.reshape(4, 2, LANES)
        return 0

    lax.fori_loop(0, tiles, step, 0, unroll=32)


def on_device(high, rest, voltages, channel_lag, offsets):
    parts, local, samp, channels = voltages.shape
    feed_count, y_count = 32, 8
    peers = feed_count * y_count
    cf = parts * local
    params = pltpu.CompilerParams(vmem_limit_bytes=VMEM_LIMIT)
    vmem = pl.BlockSpec(memory_space=pltpu.VMEM)
    smem = pl.BlockSpec(memory_space=pltpu.SMEM)

    def call(kernel, name, shape, dtype, specs, *operands):
        return pl.pallas_call(
            kernel,
            in_specs=specs,
            out_specs=vmem,
            out_shape=jax.ShapeDtypeStruct(shape, dtype),
            compiler_params=params,
            name=name,
        )(*operands)

    rows = voltages.reshape(cf, samp, channels).transpose(1, 0, 2)
    packed = call(pack_kernel, "pack", (peers, cf, LANES), jnp.bfloat16, [vmem], rows)
    turned = lax.all_to_all(packed, PEERS, split_axis=0, concat_axis=0, tiled=True)
    turned = turned.reshape(4, 8, y_count, cf, LANES)
    beams = feed_count * local
    own = call(
        beam_kernel,
        "beams",
        (2 * y_count, beams // 4, LANES),
        jnp.bfloat16,
        [vmem] * 3,
        high,
        rest,
        turned,
    )
    other = lax.ppermute(own, "core", [(0, 1), (1, 0)])
    place = lax.axis_index(PEERS).reshape(1)
    core = lax.axis_index("core").reshape(1)
    codes = call(
        tree_kernel,
        "tree",
        (4, 8, y_count, 2, LANES),
        jnp.int32,
        [smem, smem] + [vmem] * 4,
        place,
        core,
        channel_lag.reshape(-1, LANES),
        offsets,
        own,
        other,
    ).reshape(peers, 2, LANES)
    back = lax.all_to_all(codes, PEERS, split_axis=0, concat_axis=0, tiled=True)
    return call(
        unpack_kernel,
        "unpack",
        (8, 2, channels),
        jnp.float32,
        [vmem],
        back.reshape(peers // 4, 8, LANES),
    )


def solution(mesh):
    devices = mesh.devices
    fine = Mesh(devices.reshape((8, 4, 8, 2)), FEED + TIME)
    high, rest = dft_tables(8 * devices.shape[0])
    body = jax.shard_map(
        functools.partial(on_device),
        mesh=fine,
        in_specs=(P(), P(), P(None, FEED, TIME, None), P(), P()),
        out_specs=P(FEED, TIME, None),
        check_vma=False,
    )

    def run(voltages, channel_lag, offsets):
        return body(jnp.asarray(high), jnp.asarray(rest), voltages, channel_lag, offsets)

    return run
```

```python
import functools
import math

import jax
import jax.numpy as jnp
import ml_dtypes
import numpy as np
from jax import lax
from jax.experimental import pallas as pl
from jax.experimental.pallas import tpu as pltpu
from jax.sharding import Mesh
from jax.sharding import PartitionSpec as P

DS = 2
SECTIONS = 5
GROUP = 2**SECTIONS
LANES = 128
TOP = 14.5
FINE = 800.0
KNEE = -66.0
COARSE = 16.0
KNEE_CODE = (KNEE - TOP) * FINE + 65535.0
LEAST = -126.0
LEAST_CODE = int((LEAST - KNEE) * COARSE + KNEE_CODE)
VMEM_LIMIT = 48 * 1024 * 1024


def dft_tables(feeds):
    hi, big, low = np.meshgrid(np.arange(4), np.arange(feeds // 8), np.arange(2), indexing="ij")
    beam = (8 * big + 2 * hi + low).reshape(-1)
    feed = np.arange(feeds)
    angle = (beam[:, None] * feed[None, :] % feeds) * (2.0 * math.pi / feeds)
    cosine = np.cos(angle) / math.sqrt(feeds)
    sine = np.sin(angle) / math.sqrt(feeds)
    real = np.stack([cosine.reshape(feeds, -1, 8), sine.reshape(feeds, -1, 8)], axis=2)
    imag = np.stack([-sine.reshape(feeds, -1, 8), cosine.reshape(feeds, -1, 8)], axis=2)
    table = np.concatenate([real, imag], axis=0).reshape(2 * feeds, 2 * feeds)
    high = table.astype(ml_dtypes.bfloat16)
    rest = (table - high.astype(np.float64)).astype(ml_dtypes.bfloat16)
    return high, rest


def lane_index(shape):
    return lax.broadcasted_iota(jnp.int32, shape, len(shape) - 1)


def roll(x, by):
    return pltpu.roll(x, by % x.shape[-1], x.ndim - 1)


def swap_blocks(rows):
    lane = lane_index(rows[0].shape)
    low_half = lane < 64
    even = lane % 64 < 32
    turned = [rows[0]] + [roll(rows[n], 32 * n) for n in range(1, 4)]
    out = []
    for g in range(4):
        blocks = [turned[(m - g) % 4] for m in range(4)]
        mixed = jnp.where(
            low_half,
            jnp.where(even, blocks[0], blocks[1]),
            jnp.where(even, blocks[2], blocks[3]),
        )
        out.append(roll(mixed, -32 * g) if g else mixed)
    return out


def encode(x):
    level = jnp.log2(jnp.maximum(x, 2.0**LEAST))
    fine = level * FINE + (65535.5 - TOP * FINE)
    coarse = level * COARSE + (KNEE_CODE + 0.5 - KNEE * COARSE)
    return jnp.maximum(fine, coarse).astype(jnp.int32)


def decode(code):
    value = code.astype(jnp.float32)
    fine = value * (1.0 / FINE) + (TOP - 65535.0 / FINE)
    coarse = value * (1.0 / COARSE) + (KNEE - KNEE_CODE / COARSE)
    return jnp.where(code > LEAST_CODE, jnp.exp2(jnp.minimum(fine, coarse)), 0.0)


def pack_kernel(x_ref, out_ref):
    tiles = x_ref.shape[2] // LANES

    def step(j, _):
        lanes = pl.ds(pl.multiple_of(j * LANES, LANES), LANES)
        rows = [x_ref[n, :, lanes] for n in range(4)]
        for g, value in enumerate(swap_blocks(rows)):
            out_ref[4 * j + g] = value
        return 0

    lax.fori_loop(0, tiles, step, 0, unroll=16)


def beam_kernel(high_ref, rest_ref, x_ref, out_ref):
    blocks, sources, cf, lanes = x_ref.shape
    several = 2
    feeds = high_ref.shape[0] // 2
    rows = feeds // 4
    lane = lane_index((rows, lanes))
    even = lane % 64 < 32
    low_half = lane < 64
    for y in range(0, blocks, several):
        x = jnp.concatenate(
            [x_ref[y + k].reshape(sources * cf, lanes) for k in range(several)], axis=1
        )
        beam = jnp.dot(high_ref[...], x, preferred_element_type=jnp.float32)
        beam = beam + jnp.dot(rest_ref[...], x, preferred_element_type=jnp.float32)
        power = beam[:feeds] * beam[:feeds] + beam[feeds:] * beam[feeds:]
        for k in range(several):
            p = [
                power[g * rows : (g + 1) * rows, k * lanes : (k + 1) * lanes] for g in range(4)
            ]
            pairs = []
            for g in (0, 2):
                crossed = jnp.where(even, p[g + 1], p[g])
                crossed = jnp.take_along_axis(crossed, lane ^ 32, axis=1)
                pairs.append(jnp.where(even, p[g], p[g + 1]) + crossed)
            crossed = roll(jnp.where(low_half, pairs[1], pairs[0]), 64)
            first = jnp.where(low_half, pairs[0], crossed)
            second = jnp.where(low_half, crossed, pairs[1])
            out_ref[2 * (y + k)] = (first * (1.0 / DS)).astype(jnp.bfloat16)
            out_ref[2 * (y + k) + 1] = (second * (1.0 / DS)).astype(jnp.bfloat16)


def tree_kernel(place_ref, core_ref, lag_ref, off_ref, own_ref, other_ref, out_ref):
    count = own_ref.shape[0]
    times = 2 * count
    rows = 8
    lane = lane_index((rows, LANES))
    channel = lane % GROUP
    place = place_ref[0]

    per_lag = LANES // GROUP
    lag = jnp.broadcast_to(lag_ref[pl.ds(place // per_lag, 1), :], (rows, LANES))
    lag = jnp.take_along_axis(lag, (place % per_lag) * GROUP + channel, axis=1)
    half_group = GROUP // 2
    per_off = LANES // half_group
    start = pl.multiple_of(place // per_off * LANES, LANES)
    uppers, takes, partners = [], [], []
    for s in range(SECTIONS):
        h = 2**s
        values = jnp.broadcast_to(off_ref[pl.ds(s, 1), pl.ds(start, LANES)], (rows, LANES))
        pair = h * (channel // (2 * h)) + channel % h
        off = jnp.take_along_axis(values, (place % per_off) * half_group + pair, axis=1)
        upper = (channel // h) % 2 == 1
        uppers.append(upper)
        takes.append(jnp.logical_and(upper, off == 1))
        partners.append(jnp.where(upper, lane - h, lane + h))

    zero = jnp.zeros((rows, LANES), jnp.float32)

    def delay(level, late):
        return [
            jnp.where(late, level[t - 1] if t else zero, level[t]) for t in range(times)
        ]

    def run(is_odd):
        def step(k, _):
            at = pl.ds(pl.multiple_of(k * 2 * rows, 2 * rows), 2 * rows)
            for q in range(2):
                level = []
                for t in range(times):
                    mine = (t // 2) % 2 == (1 if is_odd else 0)
                    source = own_ref if mine else other_ref
                    block = source[t // 4 * 2 + t % 2, at, :].astype(jnp.float32)
                    level.append(block[q * rows : (q + 1) * rows])
                level = delay(delay(level, lag >= 1), lag >= 2)
                for s in range(SECTIONS):
                    sent = delay(level, takes[s])
                    after = []
                    for t in range(times):
                        mine = (t // 2) % 2 == (1 if is_odd else 0)
                        if s == SECTIONS - 1 and not mine:
                            after.append(None)
                            continue
                        kept = jnp.where(uppers[s], sent[t - 1] if t else zero, level[t])
                        after.append(kept + jnp.take_along_axis(sent[t], partners[s], axis=1))
                    level = after
                scale = 1.0 / 2**SECTIONS
                for y in range(count // 2):
                    t = 4 * y + (2 if is_odd else 0)
                    word = encode(level[t] * scale) | (encode(level[t + 1] * scale) << 16)
                    out_ref[y, 2 * k + q] = word
            return 0

        lax.fori_loop(0, own_ref.shape[1] // (2 * rows), step, 0)

    @pl.when(core_ref[0] == 0)
    def _():
        run(False)

    @pl.when(core_ref[0] != 0)
    def _():
        run(True)


def unpack_kernel(x_ref, out_ref):
    tiles = x_ref.shape[0]
    lane = lane_index((8, LANES))
    row = lax.broadcasted_iota(jnp.int32, (8, LANES), 0)
    stay_far = (row < 4) == (lane < 64)
    stay_near = (row % 4 < 2) == (lane % 64 < 32)

    def step(j, _):
        v = x_ref[j]
        u = jnp.where(stay_far, v, roll(pltpu.roll(v, 4, 0), 64))
        moved = jnp.take_along_axis(u, row ^ 2, axis=0)
        moved = jnp.take_along_axis(moved, lane ^ 32, axis=1)
        w = jnp.where(stay_near, u, moved)
        lanes = pl.ds(pl.multiple_of(j * LANES, LANES), LANES)
        for k in range(2):
            twice = jnp.take_along_axis(w, row // 2 + 4 * k, axis=0)
            value = decode(jnp.where(row % 2 == 1, twice >> 16, twice) & 65535)
            out_ref[4 * k : 4 * k + 4, :, lanes] = value.reshape(4, 2, LANES)
        return 0

    lax.fori_loop(0, tiles, step, 0, unroll=64)


def on_device(high, rest, voltages, channel_lag, offsets):
    parts, local, samp, channels = voltages.shape
    feed_count = lax.axis_size("feed")
    y_count = lax.axis_size("y")
    peers = feed_count * y_count
    cf = parts * local
    params = pltpu.CompilerParams(vmem_limit_bytes=VMEM_LIMIT)
    vmem = pl.BlockSpec(memory_space=pltpu.VMEM)
    smem = pl.BlockSpec(memory_space=pltpu.SMEM)

    def call(kernel, name, shape, dtype, specs, *operands):
        return pl.pallas_call(
            kernel,
            in_specs=specs,
            out_specs=vmem,
            out_shape=jax.ShapeDtypeStruct(shape, dtype),
            compiler_params=params,
            name=name,
        )(*operands)

    rows = voltages.reshape(cf, samp, channels).transpose(1, 0, 2)
    packed = call(pack_kernel, "pack", (peers, cf, LANES), jnp.bfloat16, [vmem], rows)
    turned = lax.all_to_all(packed, ("y", "feed"), split_axis=0, concat_axis=0, tiled=True)
    turned = turned.reshape(y_count, feed_count, cf, LANES)
    beams = feed_count * local
    own = call(
        beam_kernel,
        "beams",
        (2 * y_count, beams // 4, LANES),
        jnp.bfloat16,
        [vmem] * 3,
        high,
        rest,
        turned,
    )
    other = lax.ppermute(own, "core", [(0, 1), (1, 0)])
    place = (lax.axis_index("y") * feed_count + lax.axis_index("feed")).reshape(1)
    core = lax.axis_index("core").reshape(1)
    codes = call(
        tree_kernel,
        "tree",
        (y_count, feed_count // 4, 8, LANES),
        jnp.int32,
        [smem, smem] + [vmem] * 4,
        place,
        core,
        channel_lag.reshape(-1, LANES),
        offsets,
        own,
        other,
    ).reshape(peers, 2, LANES)
    back = lax.all_to_all(codes, ("y", "feed"), split_axis=0, concat_axis=0, tiled=True)
    return call(
        unpack_kernel,
        "unpack",
        (8, 2, channels),
        jnp.float32,
        [vmem],
        back.reshape(peers // 4, 8, LANES),
    )


def solution(mesh):
    devices = mesh.devices
    fine = Mesh(devices.reshape(devices.shape[0], -1, 2), ("feed", "y", "core"))
    high, rest = dft_tables(8 * devices.shape[0])
    times = ("y", "core")
    body = jax.shard_map(
        functools.partial(on_device),
        mesh=fine,
        in_specs=(P(), P(), P(None, "feed", times, None), P(), P()),
        out_specs=P("feed", times, None),
        check_vma=False,
    )

    def run(voltages, channel_lag, offsets):
        return body(jnp.asarray(high), jnp.asarray(rest), voltages, channel_lag, offsets)

    return run
```
